32 devices in a mesh: dp: 2 (over x), row: 4 (over y, core), col: 4 (over z).
Axes of the slice: x: 2, y: 2, z: 4, core: 2. Of those that a mesh axis runs over, the one named last changes fastest.
Arguments:
- tokens: bfloat16 [960, 8192], P('col', ('dp', 'row')), may hold values from -6 to 6
- attn_gain: bfloat16 [960], P('col'), may hold values from 0.5 to 1.5
- w_query: bfloat16 [960, 960], P('col', 'row'), may hold values from -0.1875 to 0.1875
- key_weight: bfloat16 [960, 320], P('col', 'row'), may hold values from -0.1875 to 0.1875
- value_weight: bfloat16 [960, 320], P('col', 'row'), may hold values from -0.1875 to 0.1875
- w_output: bfloat16 [960, 960], P('col', 'row'), may hold values from -1.5 to 1.5
- mlp_gain: bfloat16 [960], P('col'), may hold values from 0.5 to 1.5
- w_gate: bfloat16 [960, 2560], P('col', 'row'), may hold values from -0.1875 to 0.1875
- w_up: bfloat16 [960, 2560], P('col', 'row'), may hold values from -0.1875 to 0.1875
- w_down: bfloat16 [2560, 960], P('col', 'row'), may hold values from -0.125 to 0.125
- cotangent: bfloat16 [960, 8192], P('col', ('dp', 'row')), may hold values from -6 to 6
Outputs:
- output: bfloat16 [960, 8192], P('col', ('dp', 'row'))
- input_grad: float32 [960, 8192], P('col', ('dp', 'row'))
- grad_attn_gain: float32 [960], P('col')
- grad_query: float32 [960, 960], P('col', 'row')
- grad_key: float32 [960, 320], P('col', 'row')
- grad_value: float32 [960, 320], P('col', 'row')
- grad_output: float32 [960, 960], P('col', 'row')
- grad_mlp_gain: float32 [960], P('col')
- grad_gate: float32 [960, 2560], P('col', 'row')
- grad_up: float32 [960, 2560], P('col', 'row')
- grad_down: float32 [2560, 960], P('col', 'row')
The draws below stay inside these ranges and needn't reach their ends.
All inputs are finite; a program needn't handle non-finite values.
Results may differ from the reference program's by a relative error of at most 0.014.
Values may be sent and summed in bfloat16 or wider, within the bound.
No kernel may reach another device: no remote copies, remote signals or barrier semaphores. Data moves between devices by JAX's collectives and lax.ppermute only.
A program may use at most 128 MiB of HBM per device.

```python
import math
import jax
import jax.numpy as jnp
from jax import lax

MODEL_WIDTH = 960
QUERY_HEADS = 15
KEY_VALUE_HEADS = 5
HEAD_SIZE = 64
FF = 2560
SEQUENCE_TOKENS = 2048
TOKENS = 8192


def level_of(stream_key, dims, cuts, least, top_value):
    def one(axis_at, blocks):
        steps = jax.random.uniform(jax.random.fold_in(jax.random.fold_in(stream_key, 6), axis_at), (blocks,), jnp.float32, least / len(cuts), top_value / len(cuts))
        return jnp.repeat(jnp.exp(steps), dims[axis_at] // blocks).reshape((-1,) + (1,) * (len(dims) - axis_at - 1))

    level = one(*cuts[0])
    for cut in cuts[1:]:
        level = level * one(*cut)
    return level


def centred(rng, shape, scale, limit, cuts=(), kind=jnp.bfloat16):
    factor_of = level_of(rng, shape, cuts, -0.22, 0.18) if cuts else 1.0
    values = jax.random.normal(rng, shape, jnp.float32) * scale * factor_of
    return jnp.minimum(jnp.maximum(values, -limit), limit).astype(kind)


def setup_inputs(seed: int = 0) -> dict:
    keys = jax.random.split(jax.random.key(seed), 12)
    return {
        "tokens": centred(keys[0], (MODEL_WIDTH, TOKENS), 1.0, 6.0, ((0, 4), (1, 8))),
        "attn_gain": jnp.clip(1.0 + 0.1 * jax.random.normal(keys[1], (MODEL_WIDTH,), jnp.float32), 0.5, 1.5).astype(jnp.bfloat16),
        "w_query": centred(keys[2], (MODEL_WIDTH, QUERY_HEADS * HEAD_SIZE), MODEL_WIDTH ** -0.5, 0.1875, ((0, 4), (1, 4))),
        "key_weight": centred(keys[3], (MODEL_WIDTH, KEY_VALUE_HEADS * HEAD_SIZE), MODEL_WIDTH ** -0.5, 0.1875, ((0, 4), (1, 4))),
        "value_weight": centred(keys[4], (MODEL_WIDTH, KEY_VALUE_HEADS * HEAD_SIZE), MODEL_WIDTH ** -0.5, 0.1875, ((0, 4), (1, 4))),
        "w_output": centred(keys[5], (QUERY_HEADS * HEAD_SIZE, MODEL_WIDTH), (max(1, QUERY_HEADS * HEAD_SIZE // 64)) ** -0.5, 1.5, ((0, 4), (1, 4))),
        "mlp_gain": jnp.clip(1.0 + 0.1 * jax.random.normal(keys[6], (MODEL_WIDTH,), jnp.float32), 0.5, 1.5).astype(jnp.bfloat16),
        "w_gate": centred(keys[7], (MODEL_WIDTH, FF), MODEL_WIDTH ** -0.5, 0.1875, ((0, 4), (1, 4))),
        "w_up": centred(keys[8], (MODEL_WIDTH, FF), MODEL_WIDTH ** -0.5, 0.1875, ((0, 4), (1, 4))),
        "w_down": centred(keys[9], (FF, MODEL_WIDTH), FF ** -0.5, 0.125, ((0, 4), (1, 4))),
        "cotangent": centred(keys[10], (MODEL_WIDTH, TOKENS), 1.0, 6.0, ((0, 4), (1, 8))),
    }


@jax.custom_vjp
def low(v):
    return lax.optimization_barrier(v.astype(jnp.bfloat16)).astype(jnp.float32)

@jax.custom_vjp
def low_back(v):
    return v

def low_keep(v):
    return (low(v), None)

def low_pass(kept, grad):
    return (grad,)

def back_keep(v):
    return (v, None)

def back_low(kept, grad):
    return (low(grad),)
low.defvjp(low_keep, low_pass)
low_back.defvjp(back_keep, back_low)
norm_epsilon = 1e-05
rotary_base = 100000.0
masked_value = -1e+30

def matmul(left, right):
    return jnp.dot(left, right, precision=lax.Precision.HIGHEST, preferred_element_type=jnp.float32)

def rotary_tables(positions):
    half = HEAD_SIZE // 2
    inverse = rotary_base ** (-jnp.arange(half, dtype=jnp.float32) * (2.0 / HEAD_SIZE))
    angles = positions.astype(jnp.float32)[:, None] * inverse[None, :]
    return (jnp.cos(angles), jnp.sin(angles))

def rotate(value_rows, cosine, sine):
    element_count = value_rows.shape[0]
    shaped = value_rows.reshape(element_count, -1, HEAD_SIZE)
    first = shaped[:, :, :HEAD_SIZE // 2]
    second = shaped[:, :, HEAD_SIZE // 2:]
    cos_b = cosine[:, None, :]
    sin_b = sine[:, None, :]
    turned = jnp.concatenate([first * cos_b - second * sin_b, second * cos_b + first * sin_b], axis=2)
    return turned.reshape(value_rows.shape)

def normalize(value_rows, gain):
    scale = lax.rsqrt(lax.optimization_barrier(jnp.mean(value_rows * value_rows, axis=1, keepdims=True)) + norm_epsilon)
    return value_rows * scale * gain

def attend_full_sequence(parts):
    query_matrix, key, value = parts
    length = query_matrix.shape[0]
    scores = jnp.einsum('tjgd,sjd->jgts', query_matrix, key, precision=lax.Precision.HIGHEST) / math.sqrt(HEAD_SIZE)
    scores = low_back(scores)
    index = jnp.arange(length)
    causal = index[:, None] >= index[None, :]
    scores = jnp.where(causal, scores, masked_value)
    probs = low(jax.nn.softmax(scores, axis=-1))
    return jnp.einsum('jgts,sjd->tjgd', probs, value, precision=lax.Precision.HIGHEST)

def layer(inputs, attn_gain, w_query, key_weight, value_weight, w_output, mlp_gain, w_gate, w_up, w_down):
    total_tokens = inputs.shape[0]
    query_group = QUERY_HEADS // KEY_VALUE_HEADS
    element_count = total_tokens // SEQUENCE_TOKENS
    positions = jnp.arange(total_tokens) % SEQUENCE_TOKENS
    cosine, sine = rotary_tables(positions)
    act_one = low(normalize(inputs, attn_gain))
    query_pre = low_back(low(matmul(act_one, w_query)))
    key_pre = low_back(low(matmul(act_one, key_weight)))
    value_rows = low_back(low(matmul(act_one, value_weight)))
    query_matrix = low(rotate(query_pre, cosine, sine))
    key = low(rotate(key_pre, cosine, sine))
    attention_output = lax.map(jax.checkpoint(attend_full_sequence), (query_matrix.reshape(element_count, SEQUENCE_TOKENS, KEY_VALUE_HEADS, query_group, HEAD_SIZE), key.reshape(element_count, SEQUENCE_TOKENS, KEY_VALUE_HEADS, HEAD_SIZE), value_rows.reshape(element_count, SEQUENCE_TOKENS, KEY_VALUE_HEADS, HEAD_SIZE)))
    attention_output = low_back(low(attention_output.reshape(total_tokens, QUERY_HEADS * HEAD_SIZE)))
    resid = inputs + low_back(matmul(attention_output, w_output))
    act_two = low(normalize(resid, mlp_gain))
    gate = low_back(matmul(act_two, w_gate))
    upper = low_back(matmul(act_two, w_up))
    hidden = low(jax.nn.silu(gate) * upper)
    return resid + low_back(matmul(hidden, w_down))

def reference(tokens, attn_gain, w_query, key_weight, value_weight, w_output, mlp_gain, w_gate, w_up, w_down, cotangent):
    floats = tuple((item.astype(jnp.float32) for item in (tokens.T, attn_gain, w_query, key_weight, value_weight, w_output, mlp_gain, w_gate, w_up, w_down)))
    output, pullback = jax.vjp(layer, *floats)
    grads = pullback(cotangent.T.astype(jnp.float32))
    return (output.T.astype(jnp.bfloat16), grads[0].T, grads[1], grads[2], grads[3], grads[4], grads[5], grads[6], grads[7], grads[8], grads[9])
```

```python
import functools
import math

import jax
import jax.numpy as jnp
from jax import lax
from jax.experimental import pallas as pl
from jax.experimental.pallas import tpu as pltpu
from jax.sharding import PartitionSpec as P

MODEL_WIDTH = 960
QUERY_HEADS = 15
KEY_VALUE_HEADS = 5
HEAD_SIZE = 64

GROUP = QUERY_HEADS // KEY_VALUE_HEADS
KEY_VALUE_WIDTH = KEY_VALUE_HEADS * HEAD_SIZE

norm_epsilon = 1e-05
rotary_base = 100000.0
masked_value = -1e30
bf16 = jnp.bfloat16
f32 = jnp.float32


def permute(value, move, only=None):
    dp_count, row_count, col_count = (lax.axis_size(name) for name in ("dp", "row", "col"))

    def number(dp, row, col):
        return (dp * row_count + row) * col_count + col

    pairs = [
        (number(dp, row, col), number(dp ^ move[0], row ^ move[1], col ^ move[2]))
        for dp in range(dp_count)
        for row in range(row_count)
        for col in range(col_count)
        if only is None or only(dp, row, col)
    ]
    return lax.ppermute(value, ("dp", "row", "col"), pairs)


def inner_rows():
    return lax.axis_size("row") // lax.axis_size("col")


def holds(dp, row, col):
    return row // inner_rows() % 2 == dp


def lacks(dp, row, col):
    return not holds(dp, row, col)


def to_core(value):
    return permute(value, (0, 1, 0))


def to_pair(value, only):
    return permute(value, (0, inner_rows(), 0), only)


def gather_inner(value):
    count = inner_rows()
    if count == 1:
        return value
    groups = [[high * count + low for low in range(count)] for high in range(lax.axis_size("col"))]
    return lax.all_gather(value, "row", axis=1, tiled=True, axis_index_groups=groups)


def scatter_inner(value):
    count = inner_rows()
    if count == 1:
        return value
    groups = [[high * count + low for low in range(count)] for high in range(lax.axis_size("col"))]
    return lax.psum_scatter(
        value, "row", scatter_dimension=1, tiled=True, axis_index_groups=groups
    )


def xor_order(value, shift):
    count = value.shape[0]
    step = 1
    while step < count:
        shaped = value.reshape((count // (2 * step), 2, step) + value.shape[1:])
        turned = jnp.concatenate([shaped[:, 1:], shaped[:, :1]], axis=1)
        value = jnp.where((shift & step) != 0, turned, shaped).reshape(value.shape)
        step *= 2
    return value


def plane_moves(cross_pair):
    inner = inner_rows()
    return [(1, inner if cross_pair else 0, 0), (0, 2 * inner, 0)]


def plane_gather(value, moves, only=None):
    half = value.shape[0] // 2
    along = permute(value, moves[0], only)
    across = permute(value, moves[1], only)
    first = permute(across[:half], moves[0], only)
    second = permute(along[half:], moves[1], only)
    return [value, along, across, jnp.concatenate([first, second], axis=0)]


def plane_scatter(blocks, moves):
    low = [block.astype(bf16) for block in blocks]
    half = blocks[0].shape[0] // 2
    top = [block[:half] for block in blocks]
    low_top = [block[:half] for block in low]
    bottom = [block[half:] for block in blocks]
    low_bottom = [block[half:] for block in low]
    top_far = top[2] + permute(low_top[3], moves[0])
    bottom_far = bottom[1] + permute(low_bottom[3], moves[1])
    top_near = top[0] + permute(low_top[1], moves[0])
    bottom_near = bottom[0] + permute(low_bottom[2], moves[1])
    top_sum = top_near + permute(top_far.astype(bf16), moves[1])
    bottom_sum = bottom_near + permute(bottom_far.astype(bf16), moves[0])
    return jnp.concatenate([top_sum, bottom_sum], axis=0)


def plane_exchange(blocks, moves):
    result = [blocks[0]]
    for index in range(1, len(blocks)):
        move = (0, 0, 0)
        for bit, step in enumerate(moves):
            if index >> bit & 1:
                move = tuple(a ^ b for a, b in zip(move, step))
        result.append(permute(blocks[index], move))
    return result


def col_gather(value, only=None):
    return [value] + [permute(value, (0, 0, j), only) for j in range(1, lax.axis_size("col"))]


def col_scatter(blocks, only=None):
    total = blocks[0]
    for j in range(1, len(blocks)):
        total = total + permute(blocks[j].astype(bf16), (0, 0, j), only)
    return total


def swap_row_col(value, only=None):
    row_count, col_count = lax.axis_size("row"), lax.axis_size("col")
    inner = inner_rows()

    def number(dp, row, col):
        return (dp * row_count + row) * col_count + col

    pairs = [
        (number(dp, high * inner + low, col), number(dp, col * inner + low, high))
        for dp in range(lax.axis_size("dp"))
        for high in range(col_count)
        for low in range(inner)
        for col in range(col_count)
        if only is None or only(dp, col * inner + low, high)
    ]
    return lax.ppermute(value, ("dp", "row", "col"), pairs)


def is_holder():
    return lax.rem(lax.axis_index("row") // inner_rows(), 2) == lax.axis_index("dp")


def share_dp(value):
    return jnp.where(is_holder(), value, permute(value, (1, 0, 0), holds))


def share_pair(value):
    return jnp.where(is_holder(), value, to_pair(value, holds))


def spread(value):
    col_count = lax.axis_size("col")
    width, tokens = value.shape
    size = tokens // (2 * col_count)
    parts = value.reshape(width, col_count, 2, size).transpose(1, 2, 0, 3)
    got = to_core(parts[:, 1])
    both = xor_order(jnp.concatenate([parts[:, 0], got[::-1]], axis=2), lax.axis_index("col"))
    blocks = [both[0]] + [permute(both[j], (0, 0, j)) for j in range(1, col_count)]
    return jnp.concatenate(blocks, axis=0)


def unspread(value):
    col_count = lax.axis_size("col")
    width, tokens = value.shape[0] // col_count, value.shape[1]
    blocks = value.reshape(col_count, width, tokens)
    got = [blocks[0]] + [permute(blocks[j], (0, 0, j)) for j in range(1, col_count)]
    both = xor_order(jnp.stack(got), lax.axis_index("col"))
    size = tokens // 2
    other = to_core(both[::-1, :, size:])
    parts = jnp.stack([both[:, :, :size], other], axis=1)
    return parts.transpose(2, 0, 1, 3).reshape(width, col_count * tokens)


def rotary_tables(positions):
    half = HEAD_SIZE // 2
    inverse = rotary_base ** (-jnp.arange(half, dtype=f32) * (2.0 / HEAD_SIZE))
    angles = inverse[:, None] * positions.astype(f32)[None, :]
    return (jnp.cos(angles)[None], jnp.sin(angles)[None])


def rotate(value, cosine, sine):
    shaped = value.reshape(-1, 2, HEAD_SIZE // 2, value.shape[1])
    first, second = shaped[:, 0], shaped[:, 1]
    turned = jnp.stack([first * cosine - second * sine, second * cosine + first * sine], axis=1)
    return turned.reshape(value.shape)


def norm_forward(value, gain):
    scale = lax.rsqrt(jnp.sum(value * value, axis=0) / MODEL_WIDTH + norm_epsilon)
    return ((value * scale[None, :] * gain[:, None]).astype(bf16), scale)


def norm_backward(grad_normed, value, scale, gain):
    weighted = grad_normed * gain[:, None]
    inner = jnp.sum(value * weighted, axis=0)
    grad_value = (
        weighted * scale[None, :]
        - value * (scale * scale * scale * inner / MODEL_WIDTH)[None, :]
    )
    return (grad_value, jnp.sum(grad_normed * value * scale[None, :], axis=1))


def dot(left, right, left_axis, right_axis):
    return lax.dot_general(
        left, right, (((left_axis,), (right_axis,)), ((), ())), preferred_element_type=f32
    )


def chunk_blocks(core, col, col_count):
    return (col_count * core + col, col_count * (1 - core) + col_count - 1 - col)


def fill_keys(core, col, col_count, keys, values, key_s, value_s):
    size = keys[0].shape[1] // 2
    for source in range(2 * col_count):
        source_core = core if source < col_count else 1 - core
        first, second = chunk_blocks(source_core, col ^ (source % col_count), col_count)
        for refs, scratch in ((keys, key_s), (values, value_s)):
            scratch[first, :, :size] = refs[source][:, :size]
            scratch[second, :, size:] = refs[source][:, size:]


def side_by_side(ref, part, size):
    return jnp.concatenate(
        [
            ref[g * HEAD_SIZE : (g + 1) * HEAD_SIZE, part * size : (part + 1) * size]
            for g in range(GROUP)
        ],
        axis=1,
    )


def tile_allowed(shape, size, part, block, first, second):
    start = jnp.where(part == 0, first * 2 * size, second * 2 * size + size)
    lane = lax.rem(lax.broadcasted_iota(jnp.int32, shape, 1), size)
    return lax.broadcasted_iota(jnp.int32, shape, 0) - lane <= start - block * 2 * size


def attend_kernel(col_count, place, query, *refs):
    count = 2 * col_count
    keys, values = refs[:count], refs[count : 2 * count]
    output, logsum, key_s, value_s, query_s, score_s, sum_s, total_s = refs[2 * count :]
    core, col = place[0], place[1]
    size = query.shape[1] // 2
    fill_keys(core, col, col_count, keys, values, key_s, value_s)
    first, second = chunk_blocks(core, col, col_count)
    for part in range(2):
        query_s[part] = side_by_side(query, part, size)
    sum_s[...] = jnp.zeros_like(sum_s)
    total_s[...] = jnp.zeros_like(total_s)
    shape = score_s.shape[1:]
    top = [jnp.full((1, shape[1]), masked_value, f32) for _ in range(2)]
    tiles = []
    for tile in range(count + 1):
        part = (tile > first).astype(jnp.int32)
        block = tile - part * (first + 1)
        tiles.append((part, block))
        scores = dot(key_s[block], query_s[part], 0, 0)
        scores = jnp.where(
            tile_allowed(shape, size, part, block, first, second), scores, masked_value
        )
        score_s[tile] = scores
        high = jnp.max(scores, axis=0, keepdims=True)
        for side in range(2):
            top[side] = jnp.where(part == side, jnp.maximum(top[side], high), top[side])
    for tile, (part, block) in enumerate(tiles):
        weights = jnp.exp(score_s[tile] - jnp.where(part == 0, top[0], top[1]))
        total_s[part] += jnp.broadcast_to(
            jnp.sum(weights, axis=0, keepdims=True), total_s.shape[1:]
        )
        sum_s[part] += dot(value_s[block], weights.astype(bf16), 1, 0)
    for part in range(2):
        total = total_s[part][:1]
        out = (sum_s[part] * (1.0 / total)).astype(bf16)
        for g in range(GROUP):
            output[g * HEAD_SIZE : (g + 1) * HEAD_SIZE, part * size : (part + 1) * size] = out[
                :, g * size : (g + 1) * size
            ]
        logsum[0, part : part + 1, :] = top[part] + jnp.log(total)


def attend_back_kernel(col_count, place, query, grad, output, logsum, *refs):
    count = 2 * col_count
    keys, values = refs[:count], refs[count : 2 * count]
    (
        grad_query,
        grad_key_own,
        grad_value_own,
        grad_key_other,
        grad_value_other,
        key_s,
        value_s,
        query_s,
        grad_s,
        inner_s,
        sum_query,
        sum_key,
        sum_value,
    ) = refs[2 * count :]
    core, col = place[0], place[1]
    size = query.shape[1] // 2
    fill_keys(core, col, col_count, keys, values, key_s, value_s)
    first, second = chunk_blocks(core, col, col_count)
    for part in range(2):
        query_s[part] = side_by_side(query, part, size)
        grad_part = side_by_side(grad, part, size)
        grad_s[part] = grad_part
        inner = jnp.sum(
            grad_part.astype(f32) * side_by_side(output, part, size).astype(f32),
            axis=0,
            keepdims=True,
        )
        inner_s[part] = jnp.concatenate(
            [jnp.broadcast_to(inner, (8, inner.shape[1])),
             jnp.broadcast_to(logsum[0, part : part + 1, :], (8, inner.shape[1]))], axis=0
        )
    sum_query[...] = jnp.zeros_like(sum_query)
    sum_key[...] = jnp.zeros_like(sum_key)
    sum_value[...] = jnp.zeros_like(sum_value)
    shape = (2 * size, GROUP * size)
    for tile in range(count + 1):
        part = (tile > first).astype(jnp.int32)
        block = tile - part * (first + 1)
        key, value = key_s[block], value_s[block]
        query_part, grad_part = query_s[part], grad_s[part]
        inner = inner_s[part]
        scores = dot(key, query_part, 0, 0)
        probs = jnp.where(
            tile_allowed(shape, size, part, block, first, second),
            jnp.exp(jnp.minimum(scores - inner[8:9], 0.0)),
            0.0,
        )
        grad_probs = dot(value, grad_part, 0, 0)
        grad_scores = (probs * (grad_probs - inner[:1])).astype(bf16)
        sum_value[block] += dot(grad_part, probs.astype(bf16), 1, 1)
        sum_key[block] += dot(query_part, grad_scores, 1, 1)
        sum_query[part] += dot(key, grad_scores, 1, 0)
    for part in range(2):
        out = sum_query[part] * (1.0 / math.sqrt(HEAD_SIZE))
        for g in range(GROUP):
            grad_query[g * HEAD_SIZE : (g + 1) * HEAD_SIZE, part * size : (part + 1) * size] = out[
                :, g * size : (g + 1) * size
            ]
    for source in range(count):
        own = source < col_count
        source_core = core if own else 1 - core
        place_first, place_second = chunk_blocks(source_core, col ^ (source % col_count), col_count)
        index = source % col_count
        for total, target in (
            (sum_key, grad_key_own if own else grad_key_other),
            (sum_value, grad_value_own if own else grad_value_other),
        ):
            target[index, :, :size] = total[place_first][:, :size].astype(target.dtype)
            target[index, :, size:] = total[place_second][:, size:].astype(target.dtype)


def attention_specs(tokens, col_count):
    heads = pl.BlockSpec((GROUP * HEAD_SIZE, tokens), lambda h: (h, 0))
    key = pl.BlockSpec((HEAD_SIZE, tokens), lambda h: (h, 0))
    value = pl.BlockSpec((HEAD_SIZE, tokens), lambda h: (KEY_VALUE_HEADS + h, 0))
    lanes = GROUP * tokens // 2
    logsum = pl.BlockSpec((1, 2, lanes), lambda h: (h, 0, 0))
    place = pl.BlockSpec(memory_space=pltpu.SMEM)
    return heads, [key] * (2 * col_count) + [value] * (2 * col_count), logsum, place, lanes


def attend(place, query, pairs, col_count):
    tokens = query.shape[1]
    count = 2 * col_count
    heads, pair_specs, logsum, place_spec, lanes = attention_specs(tokens, col_count)
    return pl.pallas_call(
        functools.partial(attend_kernel, col_count),
        grid=(KEY_VALUE_HEADS,),
        in_specs=[place_spec, heads] + pair_specs,
        out_specs=[heads, logsum],
        out_shape=[
            jax.ShapeDtypeStruct(query.shape, bf16),
            jax.ShapeDtypeStruct((KEY_VALUE_HEADS, 2, lanes), f32),
        ],
        scratch_shapes=[
            pltpu.VMEM((count, HEAD_SIZE, tokens), bf16),
            pltpu.VMEM((count, HEAD_SIZE, tokens), bf16),
            pltpu.VMEM((2, HEAD_SIZE, lanes), bf16),
            pltpu.VMEM((count + 1, tokens, lanes), f32),
            pltpu.VMEM((2, HEAD_SIZE, lanes), f32),
            pltpu.VMEM((2, 8, lanes), f32),
        ],
        compiler_params=pltpu.CompilerParams(vmem_limit_bytes=32 * 2**20),
        cost_estimate=pl.CostEstimate(
            flops=KEY_VALUE_HEADS * (count + 1) * tokens * lanes * HEAD_SIZE * 8,
            bytes_accessed=4 * 2**20,
            transcendentals=KEY_VALUE_HEADS * (count + 1) * tokens * lanes,
        ),
        name="attend",
    )(place, query, *pairs, *pairs)


def attend_back(place, query, grad, output, logsum, pairs, col_count):
    tokens = query.shape[1]
    count = 2 * col_count
    heads, pair_specs, logsum_spec, place_spec, lanes = attention_specs(tokens, col_count)
    pair_out = pl.BlockSpec((col_count, HEAD_SIZE, tokens), lambda h: (0, h, 0))
    return pl.pallas_call(
        functools.partial(attend_back_kernel, col_count),
        grid=(KEY_VALUE_HEADS,),
        in_specs=[place_spec, heads, heads, heads, logsum_spec] + pair_specs,
        out_specs=[heads] + [pair_out] * 4,
        out_shape=[jax.ShapeDtypeStruct(query.shape, f32)]
        + [jax.ShapeDtypeStruct((col_count, KEY_VALUE_WIDTH, tokens), f32)] * 2
        + [jax.ShapeDtypeStruct((col_count, KEY_VALUE_WIDTH, tokens), bf16)] * 2,
        scratch_shapes=[
            pltpu.VMEM((count, HEAD_SIZE, tokens), bf16),
            pltpu.VMEM((count, HEAD_SIZE, tokens), bf16),
            pltpu.VMEM((2, HEAD_SIZE, lanes), bf16),
            pltpu.VMEM((2, HEAD_SIZE, lanes), bf16),
            pltpu.VMEM((2, 16, lanes), f32),
            pltpu.VMEM((2, HEAD_SIZE, lanes), f32),
            pltpu.VMEM((count, HEAD_SIZE, tokens), f32),
            pltpu.VMEM((count, HEAD_SIZE, tokens), f32),
        ],
        compiler_params=pltpu.CompilerParams(vmem_limit_bytes=32 * 2**20),
        cost_estimate=pl.CostEstimate(
            flops=KEY_VALUE_HEADS * (count + 1) * tokens * lanes * HEAD_SIZE * 20,
            bytes_accessed=8 * 2**20,
            transcendentals=KEY_VALUE_HEADS * (count + 1) * tokens * lanes,
        ),
        name="attend_back",
    )(place, query, grad, output, logsum, *pairs, *pairs)


def per_device(
    tokens,
    attn_gain,
    w_query,
    key_weight,
    value_weight,
    w_output,
    mlp_gain,
    w_gate,
    w_up,
    w_down,
    cotangent,
):
    col_count = lax.axis_size("col")
    dp, row, col = (lax.axis_index(name) for name in ("dp", "row", "col"))
    core = lax.rem(row, 2)
    high = row // inner_rows()
    plane = high - lax.rem(high, 2) + dp
    plane_count = col_count
    local_dim = tokens.shape[0]
    w_query, key_weight, value_weight, w_output, w_gate, w_up, w_down = (
        gather_inner(item)
        for item in (w_query, key_weight, value_weight, w_output, w_gate, w_up, w_down)
    )
    query_part, pair_part = w_query.shape[1], key_weight.shape[1]
    head_part = query_part + 2 * pair_part
    hidden_part = w_gate.shape[1]
    all_moves, held_moves = plane_moves(False), plane_moves(True)

    inputs = spread(tokens).astype(f32)
    qkv_block = jnp.concatenate(
        [w_query, key_weight, value_weight, attn_gain[:, None], mlp_gain[:, None]], axis=1
    )
    qkv_col = jnp.concatenate(col_gather(qkv_block, holds), axis=0)
    qkv_planes = plane_gather(qkv_col, held_moves, holds)
    qkv_own = share_pair(qkv_col)
    gains = qkv_own[:, head_part:].astype(f32)
    gain_one, gain_two = gains[:, 0], gains[:, 1]
    qkv_weight = jnp.stack([qkv_own] + [share_pair(block) for block in qkv_planes[1:]])
    qkv_weight = qkv_weight[:, :, :head_part]

    act_one, scale_one = norm_forward(inputs, gain_one)

    chunk = inputs.shape[1] // 2
    first, second = chunk_blocks(core, col, col_count)
    steps = jnp.arange(chunk)
    positions = jnp.concatenate([first * 2 * chunk + steps, second * 2 * chunk + chunk + steps])
    cosine, sine = rotary_tables(positions)

    def project(weight):
        return jnp.einsum("jdf,dt->jft", weight, act_one, preferred_element_type=f32).astype(bf16)

    kv_rel = project(qkv_weight[:, :, query_part:])
    kv_abs = xor_order(kv_rel, plane)
    key = kv_abs[:, :pair_part].reshape(KEY_VALUE_WIDTH, -1)
    value = kv_abs[:, pair_part:].reshape(KEY_VALUE_WIDTH, -1)
    key = rotate(key.astype(f32), cosine, sine).astype(bf16)
    pair = jnp.concatenate([key, value], axis=0)
    pairs = col_gather(pair)
    pairs = pairs + [to_core(block) for block in pairs]
    query = xor_order(project(qkv_weight[:, :, :query_part]), plane).reshape(MODEL_WIDTH, -1)
    query = (
        rotate(query.astype(f32), cosine, sine).astype(bf16) * (1.0 / math.sqrt(HEAD_SIZE))
    ).astype(bf16)
    place = jnp.stack([core, col]).astype(jnp.int32)
    attended, logsum = attend(place, query, pairs, col_count)

    output_block = swap_row_col(w_output.T, holds)
    output_col = jnp.concatenate(col_gather(output_block, holds), axis=0)
    output_weight = jnp.stack(
        [share_pair(block) for block in plane_gather(output_col, held_moves, holds)]
    )
    attended_rel = xor_order(attended.reshape(plane_count, query_part, -1), plane)
    resid = inputs + jnp.einsum(
        "idf,ift->dt", output_weight, attended_rel, preferred_element_type=f32
    )

    act_two, scale_two = norm_forward(resid, gain_two)
    mlp_block = jnp.stack([w_gate, w_up, swap_row_col(w_down.T, holds)])
    mlp_cols = [share_pair(block) for block in col_gather(mlp_block, holds)]
    gate_weight, up_weight, down_weight = (
        jnp.concatenate([block[index] for block in mlp_cols], axis=0) for index in range(3)
    )
    grad_top = spread(cotangent)
    grad_branch = jnp.concatenate(plane_gather(grad_top, all_moves), axis=1)
    grad_hidden = dot(down_weight, grad_branch, 0, 0)
    act_two_all = jnp.concatenate(plane_gather(act_two, all_moves), axis=1)
    gate_vals = dot(gate_weight, act_two_all, 0, 0)
    up_vals = dot(up_weight, act_two_all, 0, 0)
    sigmoid = jax.nn.sigmoid(gate_vals)
    silu_vals = gate_vals * sigmoid
    hidden = (silu_vals * up_vals).astype(bf16)
    grad_gate_vals = (
        grad_hidden * up_vals * (sigmoid * (1.0 + gate_vals * (1.0 - sigmoid)))
    ).astype(bf16)
    grad_up_vals = (grad_hidden * silu_vals).astype(bf16)
    grad_act_two_part = dot(gate_weight, grad_gate_vals, 1, 0) + dot(up_weight, grad_up_vals, 1, 0)
    size = 2 * chunk

    def token_blocks(value):
        return [value[:, i * size : (i + 1) * size] for i in range(plane_count)]

    grad_act_two = plane_scatter(token_blocks(grad_act_two_part), all_moves)
    grad_resid_norm, gain_two_part = norm_backward(grad_act_two, resid, scale_two, gain_two)
    grad_resid = grad_top.astype(f32) + grad_resid_norm
    grad_attn = grad_resid.astype(bf16)
    grad_attended = xor_order(
        jnp.einsum("idf,dt->ift", output_weight, grad_attn, preferred_element_type=f32).astype(
            bf16
        ),
        plane,
    ).reshape(MODEL_WIDTH, -1)

    down_part = dot(down_weight, hidden, 1, 0)
    output = unspread((resid + plane_scatter(token_blocks(down_part), all_moves)).astype(bf16))

    def held_sum(left, right):
        part = dot(left, right, 1, 1)
        part = part + to_pair(part.astype(bf16), lacks)
        blocks = part.reshape(col_count, -1, part.shape[1])
        return col_scatter([blocks[j] for j in range(col_count)], holds)

    grad_gate = scatter_inner(share_dp(held_sum(act_two_all, grad_gate_vals)))
    grad_up = scatter_inner(share_dp(held_sum(act_two_all, grad_up_vals)))
    grad_down = scatter_inner(swap_row_col(share_dp(held_sum(grad_branch, hidden))).T)

    attended_blocks = plane_exchange([attended_rel[i] for i in range(plane_count)], all_moves)
    grad_attn_all = jnp.concatenate(plane_gather(grad_attn, all_moves), axis=1)
    grad_output = scatter_inner(
        swap_row_col(
            share_dp(held_sum(grad_attn_all, jnp.concatenate(attended_blocks, axis=1)))
        ).T
    )

    grad_query, key_own, value_own, key_other, value_other = attend_back(
        place, query, grad_attended, attended, logsum, pairs, col_count
    )
    pair_own = jnp.concatenate([key_own, value_own], axis=1)
    pair_sum = pair_own + to_core(jnp.concatenate([key_other, value_other], axis=1))
    grad_pair = col_scatter([pair_sum[j] for j in range(col_count)])
    grad_query = rotate(grad_query, cosine, -sine).astype(bf16)
    grad_key = rotate(grad_pair[:KEY_VALUE_WIDTH], cosine, -sine).astype(bf16)
    grad_value = grad_pair[KEY_VALUE_WIDTH:].astype(bf16)
    grad_qkv = xor_order(
        jnp.concatenate(
            [
                item.reshape(plane_count, -1, item.shape[1])
                for item in (grad_query, grad_key, grad_value)
            ],
            axis=1,
        ),
        plane,
    )
    grad_act_one = jnp.einsum("jdf,jft->dt", qkv_weight, grad_qkv, preferred_element_type=f32)
    grad_inputs_norm, gain_one_part = norm_backward(grad_act_one, inputs, scale_one, gain_one)
    grad_inputs = grad_resid + grad_inputs_norm
    input_grad = unspread(grad_inputs.astype(bf16)).astype(f32)

    act_one_all = jnp.concatenate(plane_gather(act_one, all_moves), axis=1)
    grad_qkv_blocks = plane_exchange([grad_qkv[i] for i in range(plane_count)], all_moves)
    grad_heads = share_dp(held_sum(act_one_all, jnp.concatenate(grad_qkv_blocks, axis=1)))

    gain_parts = jnp.stack([gain_one_part, gain_two_part]).reshape(2, col_count, local_dim)
    gain_sum = gain_parts[:, 0]
    for j in range(1, col_count):
        gain_sum = gain_sum + permute(gain_parts[:, j], (0, 0, j))
    gain_sum = gain_sum + permute(gain_sum, (1, 0, 0))
    step = 1
    while step < lax.axis_size("row"):
        gain_sum = gain_sum + permute(gain_sum, (0, step, 0))
        step *= 2

    return (
        output,
        input_grad,
        gain_sum[0],
        scatter_inner(grad_heads[:, :query_part]),
        scatter_inner(grad_heads[:, query_part : query_part + pair_part]),
        scatter_inner(grad_heads[:, query_part + pair_part :]),
        grad_output,
        gain_sum[1],
        grad_gate,
        grad_up,
        grad_down,
    )


def solution(mesh):
    in_specs = (
        P("col", ("dp", "row")),
        P("col"),
        P("col", "row"),
        P("col", "row"),
        P("col", "row"),
        P("col", "row"),
        P("col"),
        P("col", "row"),
        P("col", "row"),
        P("col", "row"),
        P("col", ("dp", "row")),
    )
    out_specs = (
        P("col", ("dp", "row")),
        P("col", ("dp", "row")),
        P("col"),
        P("col", "row"),
        P("col", "row"),
        P("col", "row"),
        P("col", "row"),
        P("col"),
        P("col", "row"),
        P("col", "row"),
        P("col", "row"),
    )
    return jax.shard_map(
        per_device, mesh=mesh, in_specs=in_specs, out_specs=out_specs, check_vma=False
    )
```

```python
import functools
import math

import jax
import jax.numpy as jnp
import numpy as np
from jax import lax
from jax.experimental import pallas as pl
from jax.experimental.pallas import tpu as pltpu
from jax.sharding import PartitionSpec as P

MODEL_WIDTH = 960
QUERY_HEADS = 15
KEY_VALUE_HEADS = 5
HEAD_SIZE = 64

GROUP = QUERY_HEADS // KEY_VALUE_HEADS
KEY_VALUE_WIDTH = KEY_VALUE_HEADS * HEAD_SIZE

norm_epsilon = 1e-05
rotary_base = 100000.0
masked_value = -1e30
bf16 = jnp.bfloat16
f32 = jnp.float32


class Axes:
    def __init__(self, mesh):
        shape = dict(mesh.shape)
        inner = shape["row"] // 4
        if inner == 1:
            names, sizes = ("dp", "hi", "core", "col"), (shape["dp"], 2, 2, shape["col"])
            self.pair, self.inner = "core", ()
        else:
            names = ("dp", "hi", "pair", "inner", "core", "col")
            sizes = (shape["dp"], 2, 2, inner // 2, 2, shape["col"])
            self.pair, self.inner = "pair", ("inner", "core")
        self.mesh = jax.sharding.Mesh(mesh.devices.reshape(sizes), names)
        self.names, self.sizes, self.inner_count = names, sizes, inner
        self.rows = names[1:-1]
        self.quarter = ("hi", self.pair)

    def flip(self, value, *flipped):
        grid = np.arange(math.prod(self.sizes)).reshape(self.sizes)
        for name in flipped:
            grid = np.flip(grid, self.names.index(name))
        return lax.ppermute(value, self.names, list(enumerate(grid.ravel().tolist())))

    def swap(self, value):
        grid = np.arange(math.prod(self.sizes)).reshape(self.sizes[0], 4, -1, 4)
        return lax.ppermute(
            value, self.names, list(enumerate(grid.transpose(0, 3, 2, 1).ravel().tolist()))
        )

    def gather_inner(self, value):
        return lax.all_gather(value, self.inner, axis=1, tiled=True) if self.inner else value

    def scatter_inner(self, value):
        if not self.inner:
            return value
        return lax.psum_scatter(value, self.inner, scatter_dimension=1, tiled=True)

    def gather_quarter(self, value):
        far = self.flip(value, "hi")
        near = self.flip(jnp.stack([value, far]), self.pair)
        return [value, near[0], far, near[1]]

    def scatter_quarter(self, blocks):
        near = self.flip(jnp.stack([blocks[1], blocks[3]]).astype(bf16), self.pair)
        far = self.flip((blocks[2] + near[1]).astype(bf16), "hi")
        return blocks[0] + near[0] + far

    def col_xor(self, value, step):
        grid = np.arange(math.prod(self.sizes)).reshape(-1, self.sizes[-1])
        other = grid[:, np.arange(self.sizes[-1]) ^ step]
        return lax.ppermute(value, self.names, list(zip(grid.ravel().tolist(), other.ravel().tolist())))

    def gather_col_steps(self, value):
        far = self.col_xor(value, 2)
        near = self.col_xor(jnp.stack([value, far]), 1)
        return [value, near[0], far, near[1]]

    def scatter_col_steps(self, part):
        blocks = part.reshape(self.sizes[-1], -1, part.shape[1])
        near = self.col_xor(jnp.stack([blocks[1], blocks[3]]).astype(bf16), 1)
        far = self.col_xor((blocks[2] + near[1]).astype(bf16), 2)
        return blocks[0] + near[0] + far

    def dp_sum(self, value):
        return value + self.flip(value.astype(bf16), "dp")

    def exchange_quarter(self, blocks):
        return [
            blocks[0],
            self.flip(blocks[1], self.pair),
            self.flip(blocks[2], "hi"),
            self.flip(blocks[3], "hi", self.pair),
        ]

    def gather_col(self, value):
        count = self.sizes[-1]
        return lax.all_to_all(jnp.broadcast_to(value[None], (count,) + value.shape), "col", 0, 0)

    def by_dp(self, first, second):
        return jnp.where(lax.axis_index("dp") == 0, first, second)

    def gather_half(self, value):
        parts = value.reshape(2, -1, value.shape[1])
        return lax.all_gather(self.by_dp(parts[0], parts[1]), "col", axis=0)

    def whole_rows(self, mine, other):
        return self.by_dp(jnp.concatenate([mine, other]), jnp.concatenate([other, mine]))

    def both_halves(self, mine, other):
        both = self.by_dp(jnp.stack([mine, other], axis=1), jnp.stack([other, mine], axis=1))
        return both.reshape(-1, mine.shape[-1])

    def spread(self, *values):
        count = self.sizes[-1]
        width, tokens = values[0].shape
        parts = jnp.stack(values).reshape(len(values), width, 2 * count, -1)
        parts = jnp.where(lax.axis_index("core") == 1, parts[:, :, ::-1], parts)
        parts = parts.reshape(len(values), width, count, 2, -1).transpose(3, 2, 0, 1, 4)
        parts = parts.reshape((2 * count,) + parts.shape[2:])
        got = lax.all_to_all(parts, ("core", "col"), 0, 0)
        got = got.reshape((2, count) + got.shape[1:])
        return [
            jnp.concatenate([got[part, :, i].reshape(count * width, -1) for part in range(2)], axis=1)
            for i in range(len(values))
        ]

    def unspread(self, gains, *values):
        count, many, rows = self.sizes[-1], len(values), gains.shape[0]
        width, size = values[0].shape[0] // count, values[0].shape[1] // 2
        extra_rows = -(-rows * width // (16 * size)) * 16
        extra = gains.astype(bf16).reshape(rows, count, width).transpose(1, 0, 2)
        extra = jnp.pad(
            extra.reshape(count, -1), ((0, 0), (0, extra_rows * size - rows * width))
        ).reshape(count, extra_rows, size)
        parts = jnp.stack(
            [
                jnp.concatenate(
                    [
                        value[j * width : (j + 1) * width, part * size : (part + 1) * size]
                        for value in values
                    ]
                    + [extra[j]]
                )
                for part in range(2)
                for j in range(count)
            ]
        )
        got = lax.all_to_all(parts, ("core", "col"), 0, 0)
        turn = lax.axis_index("core") == 1
        outs = []
        for i in range(many):
            pieces = [got[k * count + j, i * width : (i + 1) * width] for j in range(count) for k in range(2)]
            pieces = [jnp.where(turn, pieces[-1 - j], pieces[j]) for j in range(2 * count)]
            outs.append(jnp.concatenate(pieces, axis=1))
        extra = jnp.sum(got[:, many * width :].astype(f32), axis=0)
        return outs + [extra.reshape(-1)[: rows * width].reshape(rows, width)]


def after(value, *others):
    return lax.optimization_barrier((value,) + others)[0]


together = lax.optimization_barrier


def xor_blocks(blocks, shift):
    step = 1
    while step < len(blocks):
        turn = (shift & step) != 0
        blocks = [jnp.where(turn, blocks[i ^ step], blocks[i]) for i in range(len(blocks))]
        step *= 2
    return blocks


def xor_order(value, shift):
    return jnp.stack(xor_blocks(list(value), shift))


def xor_rows(value, shift):
    return jnp.concatenate(xor_blocks(jnp.split(value, 4), shift))


def rotary_tables(positions):
    half = HEAD_SIZE // 2
    inverse = rotary_base ** (-jnp.arange(half, dtype=f32) * (2.0 / HEAD_SIZE))
    angles = inverse[:, None] * positions.astype(f32)[None, :]
    return (jnp.cos(angles)[None], jnp.sin(angles)[None])


def rotate(value, cosine, sine):
    shaped = value.reshape(-1, 2, HEAD_SIZE // 2, value.shape[1])
    first, second = shaped[:, 0], shaped[:, 1]
    turned = jnp.stack([first * cosine - second * sine, second * cosine + first * sine], axis=1)
    return turned.reshape(value.shape)


def norm_forward(value, gain):
    scale = lax.rsqrt(jnp.sum(value * value, axis=0) / MODEL_WIDTH + norm_epsilon)
    return ((value * scale[None, :] * gain[:, None]).astype(bf16), scale)


def norm_backward(grad_normed, value, scale, gain):
    weighted = grad_normed * gain[:, None]
    inner = jnp.sum(value * weighted, axis=0)
    grad_value = (
        weighted * scale[None, :]
        - value * (scale * scale * scale * inner / MODEL_WIDTH)[None, :]
    )
    return (grad_value, jnp.sum(grad_normed * value * scale[None, :], axis=1))


def dot(left, right, left_axis, right_axis):
    return lax.dot_general(
        left, right, (((left_axis,), (right_axis,)), ((), ())), preferred_element_type=f32
    )


def chunk_blocks(core, col, col_count):
    return ((col, core), (2 * col_count - 1 - col, 1 - core))


def fill_keys(core, col, col_count, own, other, key_s, value_s):
    size = own.shape[3] // 2
    for j in range(col_count):
        for ref, source in ((own, core), (other, 1 - core)):
            for part, (block, side) in enumerate(chunk_blocks(source, col ^ j, col_count)):
                key_s[block, side] = ref[j, 0, :, part * size : (part + 1) * size]
                value_s[block, side] = ref[j, 1, :, part * size : (part + 1) * size]


def both_sides(scratch, block):
    return jnp.concatenate([scratch[block, 0], scratch[block, 1]], axis=1)


def side_by_side(ref, part, size):
    return jnp.concatenate(
        [
            ref[g * HEAD_SIZE : (g + 1) * HEAD_SIZE, part * size : (part + 1) * size]
            for g in range(GROUP)
        ],
        axis=1,
    )


def tile_allowed(shape, size, part, block, early, late):
    start = jnp.where(part == 0, 2 * early[0] + early[1], 2 * late[0] + late[1]) * size
    lane = lax.rem(lax.broadcasted_iota(jnp.int32, shape, 1), size)
    return lax.broadcasted_iota(jnp.int32, shape, 0) - lane <= start - block * 2 * size


def attend_kernel(col_count, place, query, own, other, output, logsum, *scratch):
    key_s, value_s, query_s, score_s, sum_s, total_s = scratch
    core, col = place[0], place[1]
    size = query.shape[1] // 2
    fill_keys(core, col, col_count, own, other, key_s, value_s)
    early, late = chunk_blocks(core, col, col_count)
    for part in range(2):
        query_s[part] = side_by_side(query, part, size)
    sum_s[...] = jnp.zeros_like(sum_s)
    total_s[...] = jnp.zeros_like(total_s)
    shape = score_s.shape[1:]
    top = [jnp.full((1, shape[1]), masked_value, f32) for _ in range(2)]
    tiles = []
    for tile in range(2 * col_count + 1):
        part = (tile > early[0]).astype(jnp.int32)
        block = tile - part * (early[0] + 1)
        tiles.append((part, block))
        scores = dot(both_sides(key_s, block), query_s[part], 0, 0)
        scores = jnp.where(
            tile_allowed(shape, size, part, block, early, late), scores, masked_value
        )
        score_s[tile] = scores
        high = jnp.max(scores, axis=0, keepdims=True)
        for side in range(2):
            top[side] = jnp.where(part == side, jnp.maximum(top[side], high), top[side])
    for tile, (part, block) in enumerate(tiles):
        weights = jnp.exp(score_s[tile] - jnp.where(part == 0, top[0], top[1]))
        total_s[part] += jnp.broadcast_to(
            jnp.sum(weights, axis=0, keepdims=True), total_s.shape[1:]
        )
        sum_s[part] += dot(both_sides(value_s, block), weights.astype(bf16), 1, 0)
    for part in range(2):
        total = total_s[part][:1]
        out = (sum_s[part] * (1.0 / total)).astype(bf16)
        for g in range(GROUP):
            output[g * HEAD_SIZE : (g + 1) * HEAD_SIZE, part * size : (part + 1) * size] = out[
                :, g * size : (g + 1) * size
            ]
        logsum[0, part : part + 1, :] = top[part] + jnp.log(total)


def attend_back_kernel(col_count, place, query, grad, output, logsum, own, other, *refs):
    grad_query, grad_own, grad_other = refs[:3]
    key_s, value_s, query_s, grad_s, inner_s, sum_query, sum_key, sum_value = refs[3:]
    core, col = place[0], place[1]
    size = query.shape[1] // 2
    fill_keys(core, col, col_count, own, other, key_s, value_s)
    early, late = chunk_blocks(core, col, col_count)
    for part in range(2):
        query_s[part] = side_by_side(query, part, size)
        grad_part = side_by_side(grad, part, size)
        grad_s[part] = grad_part
        inner = jnp.sum(
            grad_part.astype(f32) * side_by_side(output, part, size).astype(f32),
            axis=0,
            keepdims=True,
        )
        wide = (8, inner.shape[1])
        inner_s[part] = jnp.concatenate(
            [
                jnp.broadcast_to(inner, wide),
                jnp.broadcast_to(logsum[0, part : part + 1, :], wide),
            ],
            axis=0,
        )
    sum_query[...] = jnp.zeros_like(sum_query)
    sum_key[...] = jnp.zeros_like(sum_key)
    sum_value[...] = jnp.zeros_like(sum_value)
    shape = (2 * size, GROUP * size)
    for tile in range(2 * col_count + 1):
        part = (tile > early[0]).astype(jnp.int32)
        block = tile - part * (early[0] + 1)
        key, value = both_sides(key_s, block), both_sides(value_s, block)
        query_part, grad_part = query_s[part], grad_s[part]
        inner = inner_s[part]
        scores = jnp.where(
            tile_allowed(shape, size, part, block, early, late),
            dot(key, query_part, 0, 0),
            masked_value,
        )
        probs = jnp.exp(scores - inner[8:9])
        grad_probs = dot(value, grad_part, 0, 0)
        grad_scores = (probs * (grad_probs - inner[:1])).astype(bf16)
        sum_value[block] += dot(grad_part, probs.astype(bf16), 1, 1)
        sum_key[block] += dot(query_part, grad_scores, 1, 1)
        sum_query[part] += dot(key, grad_scores, 1, 0)
    for part in range(2):
        out = sum_query[part] * (1.0 / math.sqrt(HEAD_SIZE))
        for g in range(GROUP):
            grad_query[g * HEAD_SIZE : (g + 1) * HEAD_SIZE, part * size : (part + 1) * size] = out[
                :, g * size : (g + 1) * size
            ]
    for j in range(col_count):
        for ref, source in ((grad_own, core), (grad_other, 1 - core)):
            for part, (block, side) in enumerate(chunk_blocks(source, col ^ j, col_count)):
                for index, total in enumerate((sum_key, sum_value)):
                    whole = total[block]
                    ref[j, index, :, part * size : (part + 1) * size] = jnp.where(
                        side == 0, whole[:, :size], whole[:, size:]
                    ).astype(ref.dtype)


def attention_specs(tokens, col_count):
    heads = pl.BlockSpec((GROUP * HEAD_SIZE, tokens), lambda h: (h, 0))
    pair = pl.BlockSpec((col_count, 2, HEAD_SIZE, tokens), lambda h: (0, 0, h, 0))
    lanes = GROUP * tokens // 2
    logsum = pl.BlockSpec((1, 2, lanes), lambda h: (h, 0, 0))
    place = pl.BlockSpec(memory_space=pltpu.SMEM)
    keys = [pltpu.VMEM((2 * col_count, 2, HEAD_SIZE, tokens // 2), bf16)] * 2
    return heads, pair, logsum, place, lanes, keys


def attend(place, query, own, other, col_count):
    tokens = query.shape[1]
    count = 2 * col_count
    heads, pair, logsum, place_spec, lanes, keys = attention_specs(tokens, col_count)
    return pl.pallas_call(
        functools.partial(attend_kernel, col_count),
        grid=(KEY_VALUE_HEADS,),
        in_specs=[place_spec, heads, pair, pair],
        out_specs=[heads, logsum],
        out_shape=[
            jax.ShapeDtypeStruct(query.shape, bf16),
            jax.ShapeDtypeStruct((KEY_VALUE_HEADS, 2, lanes), f32),
        ],
        scratch_shapes=keys
        + [
            pltpu.VMEM((2, HEAD_SIZE, lanes), bf16),
            pltpu.VMEM((count + 1, tokens, lanes), f32),
            pltpu.VMEM((2, HEAD_SIZE, lanes), f32),
            pltpu.VMEM((2, 8, lanes), f32),
        ],
        compiler_params=pltpu.CompilerParams(vmem_limit_bytes=32 * 2**20),
        cost_estimate=pl.CostEstimate(
            flops=KEY_VALUE_HEADS * (count + 1) * tokens * lanes * HEAD_SIZE * 8,
            bytes_accessed=4 * 2**20,
            transcendentals=KEY_VALUE_HEADS * (count + 1) * tokens * lanes,
        ),
        name="attend",
    )(place, query, own, other)


def attend_back(place, query, grad, output, logsum, own, other, col_count):
    tokens = query.shape[1]
    count = 2 * col_count
    heads, pair, logsum_spec, place_spec, lanes, keys = attention_specs(tokens, col_count)
    return pl.pallas_call(
        functools.partial(attend_back_kernel, col_count),
        grid=(KEY_VALUE_HEADS,),
        in_specs=[place_spec, heads, heads, heads, logsum_spec, pair, pair],
        out_specs=[heads, pair, pair],
        out_shape=[
            jax.ShapeDtypeStruct(query.shape, f32),
            jax.ShapeDtypeStruct(own.shape, f32),
            jax.ShapeDtypeStruct(own.shape, bf16),
        ],
        scratch_shapes=keys
        + [
            pltpu.VMEM((2, HEAD_SIZE, lanes), bf16),
            pltpu.VMEM((2, HEAD_SIZE, lanes), bf16),
            pltpu.VMEM((2, 16, lanes), f32),
            pltpu.VMEM((2, HEAD_SIZE, lanes), f32),
            pltpu.VMEM((count, HEAD_SIZE, tokens), f32),
            pltpu.VMEM((count, HEAD_SIZE, tokens), f32),
        ],
        compiler_params=pltpu.CompilerParams(vmem_limit_bytes=32 * 2**20),
        cost_estimate=pl.CostEstimate(
            flops=KEY_VALUE_HEADS * (count + 1) * tokens * lanes * HEAD_SIZE * 20,
            bytes_accessed=8 * 2**20,
            transcendentals=KEY_VALUE_HEADS * (count + 1) * tokens * lanes,
        ),
        name="attend_back",
    )(place, query, grad, output, logsum, own, other)


def per_device(
    axes,
    tokens,
    attn_gain,
    w_query,
    key_weight,
    value_weight,
    w_output,
    mlp_gain,
    w_gate,
    w_up,
    w_down,
    cotangent,
):
    col_count = axes.sizes[-1]
    core, col = lax.axis_index("core"), lax.axis_index("col")
    quarter = lax.axis_index("hi") * 2 + lax.axis_index(axes.pair)
    w_query, key_weight, value_weight, w_output, w_gate, w_up, w_down = (
        axes.gather_inner(item)
        for item in (w_query, key_weight, value_weight, w_output, w_gate, w_up, w_down)
    )
    local_dim = tokens.shape[0]
    query_part, pair_part = w_query.shape[1], key_weight.shape[1]
    hidden_part = w_gate.shape[1]

    (inputs,) = axes.spread(tokens)
    inputs = inputs.astype(f32)
    down_block = axes.swap(w_down.T)
    pair_block = jnp.concatenate(
        [key_weight, value_weight, attn_gain[:, None], mlp_gain[:, None]], axis=1
    )
    pair_col = jnp.concatenate(xor_blocks(axes.gather_col_steps(pair_block), col))
    inputs, pair_col, down_block = together((inputs, pair_col, down_block))
    gains = pair_col[:, 2 * pair_part :].astype(f32)
    gain_one, gain_two = gains[:, 0], gains[:, 1]

    tokens_here = inputs.shape[1]
    (grad_top,) = axes.spread(after(cotangent, inputs))
    wide_block = after(jnp.concatenate([w_query, w_output], axis=1), pair_col)
    act_one, scale_one = norm_forward(inputs, gain_one)
    pair_far, wide_far, act_one = together(
        (axes.flip(pair_col, "hi"), axes.col_xor(wide_block, 2), act_one)
    )

    size = tokens_here // 2
    steps = jnp.arange(size)
    early, late = chunk_blocks(core, col, col_count)
    positions = jnp.concatenate(
        [(2 * early[0] + early[1]) * size + steps, (2 * late[0] + late[1]) * size + steps]
    )
    cosine, sine = rotary_tables(positions)
    wide_near = axes.col_xor(jnp.stack([wide_block, wide_far]), 1)
    pair_near = axes.flip(jnp.stack([pair_col, pair_far]), axes.pair)
    pair_weight = jnp.stack([pair_col, pair_near[0], pair_far, pair_near[1]])
    pair_weight = pair_weight[:, :, : 2 * pair_part]
    pair = xor_order(
        jnp.einsum("jdf,dt->jft", pair_weight, act_one, preferred_element_type=f32).astype(bf16),
        quarter,
    )
    key = pair[:, :pair_part].reshape(KEY_VALUE_WIDTH, -1)
    value = pair[:, pair_part:].reshape(KEY_VALUE_WIDTH, -1)
    key = rotate(key.astype(f32), cosine, sine).astype(bf16)
    pair, wide_near, grad_top = together((jnp.stack([key, value]), wide_near, grad_top))
    wide_col = xor_blocks([wide_block, wide_near[0], wide_far, wide_near[1]], col)
    query_col = jnp.concatenate([block[:, :query_part] for block in wide_col])
    output_col = jnp.concatenate([block[:, query_part:] for block in wide_col])
    query_col, output_col = together((query_col, output_col))

    gate_up_mine = axes.gather_half(after(jnp.concatenate([w_gate, w_up], axis=1), pair))
    pair_z_far, query_far = together((axes.col_xor(pair, 2), axes.flip(query_col, "hi")))

    query_near = axes.flip(jnp.stack([query_col, query_far]), axes.pair)
    query_weight = jnp.stack([query_col, query_near[0], query_far, query_near[1]])
    query = xor_order(
        jnp.einsum("jdf,dt->jft", query_weight, act_one, preferred_element_type=f32).astype(bf16),
        quarter,
    ).reshape(MODEL_WIDTH, -1)
    query = (
        rotate(query.astype(f32), cosine, sine).astype(bf16) * (1.0 / math.sqrt(HEAD_SIZE))
    ).astype(bf16)
    pair_z_near, output_far, query = together(
        (
            axes.col_xor(jnp.stack([pair, pair_z_far]), 1),
            axes.flip(after(output_col, query_far), "hi"),
            query,
        )
    )

    down_weight = lax.all_gather(after(down_block, query), "col", axis=0, tiled=True)
    own = jnp.stack([pair, pair_z_near[0], pair_z_far, pair_z_near[1]])
    other, output_near = together(
        (
            axes.flip(own, "core"),
            axes.flip(jnp.stack([output_col, output_far]), axes.pair),
        )
    )
    output_weight = jnp.stack(
        xor_blocks([output_col, output_near[0], output_far, output_near[1]], quarter)
    )

    place = jnp.stack([core, col]).astype(jnp.int32)
    attended, logsum = attend(place, query, own, other, col_count)
    gate_up_other = axes.flip(after(gate_up_mine, query), "dp")
    attended, grad_far = together((attended, axes.flip(after(grad_top, other), "hi")))

    resid = inputs + jnp.einsum(
        "rfd,ft->rdt", output_weight, attended, preferred_element_type=f32
    ).reshape(inputs.shape)
    act_two, scale_two = norm_forward(resid, gain_two)
    grad_near = axes.flip(jnp.stack([grad_top, grad_far]), axes.pair)
    act_two, act_two_far, grad_near, gate_up_other = together(
        (act_two, axes.flip(act_two, "hi"), grad_near, gate_up_other)
    )
    gate_up_weight = axes.both_halves(gate_up_mine, gate_up_other)
    grad_branch = jnp.concatenate([grad_top, grad_near[0], grad_far, grad_near[1]], axis=1)
    act_two_near, gate_up_weight, grad_branch, down_weight = together(
        (
            axes.flip(jnp.stack([act_two, act_two_far]), axes.pair),
            gate_up_weight,
            grad_branch,
            down_weight,
        )
    )

    act_two_all = jnp.concatenate(
        [act_two, act_two_near[0], act_two_far, act_two_near[1]], axis=1
    )
    act_two_all = lax.optimization_barrier(act_two_all)
    grad_hidden = dot(down_weight, grad_branch, 0, 0)
    gate_up_vals = dot(gate_up_weight, act_two_all, 0, 0)
    gate_vals, up_vals = gate_up_vals[:hidden_part], gate_up_vals[hidden_part:]
    sigmoid = jax.nn.sigmoid(gate_vals)
    silu_vals = gate_vals * sigmoid
    hidden = (silu_vals * up_vals).astype(bf16)
    grad_gate_up = jnp.concatenate(
        [
            grad_hidden * up_vals * (sigmoid * (1.0 + gate_vals * (1.0 - sigmoid))),
            grad_hidden * silu_vals,
        ],
        axis=0,
    ).astype(bf16)
    hidden, grad_gate_up = together((hidden, grad_gate_up))

    def token_blocks(value):
        return [value[:, i * tokens_here : (i + 1) * tokens_here] for i in range(4)]

    parts = token_blocks(dot(gate_up_weight, grad_gate_up, 1, 0))
    near = axes.flip(jnp.stack([parts[1], parts[3]]).astype(bf16), axes.pair)
    act_two_rel = lax.optimization_barrier(xor_rows(act_two_all, col))
    gate_up_part = dot(act_two_rel, grad_gate_up, 1, 1)
    gate_up_part = gate_up_part.reshape(col_count, local_dim, -1)
    gate_up_low = jnp.stack([gate_up_part[1], gate_up_part[3]]).astype(bf16)
    near, gate_up_low = together((near, gate_up_low))
    gate_up_near = axes.col_xor(gate_up_low, 1)
    down_w_part = dot(grad_branch, hidden, 1, 1).astype(bf16)
    far, down_w_part = together(
        (axes.flip((parts[2] + near[1]).astype(bf16), "hi"), down_w_part)
    )
    down_sum = lax.psum_scatter(down_w_part, "col", scatter_dimension=0, tiled=True)
    grad_act_two = parts[0] + near[0] + far
    grad_resid_norm, gain_two_part = norm_backward(grad_act_two, resid, scale_two, gain_two)
    grad_resid = grad_top.astype(f32) + grad_resid_norm
    grad_attn = grad_resid.astype(bf16)
    grad_attended = jnp.einsum(
        "rfd,rdt->ft",
        output_weight,
        grad_attn.reshape(4, -1, tokens_here),
        preferred_element_type=f32,
    ).astype(bf16)

    both = jnp.stack([act_one, grad_attn])
    both_far = axes.flip(both, "hi")
    grad_query, grad_own, grad_other = attend_back(
        place, query, grad_attended, attended, logsum, own, other, col_count
    )
    grad_other, gate_up_near = together((grad_other, gate_up_near))
    gate_up_low = (gate_up_part[2] + gate_up_near[1]).astype(bf16)
    grad_pair = grad_own + axes.flip(grad_other, "core")
    pair_low = jnp.stack([grad_pair[1], grad_pair[3]]).astype(bf16)
    pair_low, gate_up_low = together((pair_low, gate_up_low))

    grad_query = rotate(grad_query, cosine, -sine).astype(bf16)
    query_rel = xor_order(grad_query.reshape(4, -1, tokens_here), quarter)
    parts = token_blocks(dot(down_weight, after(hidden, pair_low), 1, 0))
    near = axes.flip(jnp.stack([parts[1], parts[3]]).astype(bf16), axes.pair)
    attended_rel = xor_order(attended.reshape(4, -1, tokens_here), quarter)
    sent = jnp.concatenate([query_rel, attended_rel], axis=1)
    pair_near, near, head_all, both_far, gate_up_far = together(
        (
            axes.col_xor(pair_low, 1),
            near,
            axes.exchange_quarter(list(after(sent, pair_low))),
            both_far,
            axes.col_xor(gate_up_low, 2),
        )
    )
    both_near = axes.flip(jnp.stack([both, both_far]), axes.pair)
    pair_low = (grad_pair[2] + pair_near[1]).astype(bf16)
    head_all = jnp.concatenate(head_all, axis=1)
    act_one_all, grad_attn_all = (
        jnp.concatenate(
            [both[i], both_near[0, i], both_far[i], both_near[1, i]], axis=1
        )
        for i in range(2)
    )
    act_one_rel, grad_attn_rel = together(
        (xor_rows(act_one_all, col), xor_rows(grad_attn_all, col))
    )
    grad_query_w = dot(act_one_rel, head_all[:query_part], 1, 1)
    grad_output_w = dot(grad_attn_rel, head_all[query_part:], 1, 1)
    grad_act_one = jnp.einsum(
        "jdf,jft->dt", query_weight, after(query_rel, pair_low), preferred_element_type=f32
    )
    early_part = jnp.concatenate([grad_query_w, grad_output_w], axis=1)
    early_part = early_part.reshape(col_count, 2, local_dim // 2, -1)
    early_sent = axes.by_dp(early_part[:, 1], early_part[:, 0]).astype(bf16)
    early_kept = axes.by_dp(early_part[:, 0], early_part[:, 1])
    pair_far, far, early_got, early_kept, grad_act_one, act_one_rel = together(
        (
            axes.col_xor(pair_low, 2),
            axes.flip((parts[2] + near[1]).astype(bf16), "hi"),
            axes.flip(early_sent, "dp"),
            early_kept,
            grad_act_one,
            act_one_rel,
        )
    )
    early_part = early_kept + early_got
    output = (resid + (parts[0] + near[0] + far)).astype(bf16)
    grad_pair = grad_pair[0] + pair_near[0] + pair_far

    grad_key = rotate(grad_pair[0], cosine, -sine).astype(bf16)
    grad_value = grad_pair[1].astype(bf16)
    pair_rel = xor_order(
        jnp.concatenate(
            [grad_key.reshape(4, -1, tokens_here), grad_value.reshape(4, -1, tokens_here)], axis=1
        ),
        quarter,
    )
    grad_act_one = grad_act_one + jnp.einsum(
        "jdf,jft->dt", pair_weight, pair_rel, preferred_element_type=f32
    )
    grad_inputs_norm, gain_one_part = norm_backward(grad_act_one, inputs, scale_one, gain_one)
    grad_inputs = (grad_resid + grad_inputs_norm).astype(bf16)
    pair_all, grad_inputs = together((axes.exchange_quarter(list(pair_rel)), grad_inputs))
    output, input_grad, gain_sum = axes.unspread(
        jnp.stack([gain_one_part, gain_two_part]), output, grad_inputs
    )
    early_near = axes.col_xor(
        after(jnp.stack([early_part[1], early_part[3]]).astype(bf16), grad_inputs), 1
    )
    grad_pair_w = dot(act_one_rel, jnp.concatenate(pair_all, axis=1), 1, 1)
    late_part = grad_pair_w.reshape(col_count, local_dim, -1)
    gate_up_total = gate_up_part[0] + gate_up_near[0] + gate_up_far
    late_near, early_near, gate_up_dp = together(
        (
            axes.col_xor(jnp.stack([late_part[1], late_part[3]]).astype(bf16), 1),
            early_near,
            axes.flip(after(gate_up_total.astype(bf16), grad_inputs), "dp"),
        )
    )
    late_far, early_far, down_sum = together(
        (
            axes.col_xor((late_part[2] + late_near[1]).astype(bf16), 2),
            axes.col_xor((early_part[2] + early_near[1]).astype(bf16), 2),
            axes.swap(after(down_sum, grad_inputs)),
        )
    )
    late_sum = late_part[0] + late_near[0] + late_far
    early_sum = (early_part[0] + early_near[0] + early_far).astype(bf16)
    query_half, output_half = early_sum[:, :query_part], early_sum[:, query_part:]
    late_dp, down_dp, query_dp, output_half = together(
        (
            axes.flip(late_sum.astype(bf16), "dp"),
            axes.flip(down_sum, "dp"),
            axes.flip(query_half, "dp"),
            axes.swap(output_half),
        )
    )
    output_dp = axes.flip(output_half, "dp")
    gain_sum = gain_sum + axes.flip(gain_sum, "hi")
    gain_sum = gain_sum + axes.flip(gain_sum, "dp")
    for name in axes.rows[1:-1]:
        gain_sum = lax.psum(gain_sum, name)
    grad_gate_up_w = gate_up_total + gate_up_dp
    grad_pair_w = late_sum + late_dp
    grad_query_w = axes.whole_rows(query_half, query_dp).astype(f32)
    grad_output = axes.whole_rows(output_half, output_dp).T.astype(f32)
    grad_output = axes.scatter_inner(grad_output)
    grad_down = axes.scatter_inner((down_sum.astype(f32) + down_dp).T)

    return (
        output,
        input_grad.astype(f32),
        gain_sum[0],
        axes.scatter_inner(grad_query_w),
        axes.scatter_inner(grad_pair_w[:, :pair_part]),
        axes.scatter_inner(grad_pair_w[:, pair_part:]),
        grad_output,
        gain_sum[1],
        axes.scatter_inner(grad_gate_up_w[:, :hidden_part]),
        axes.scatter_inner(grad_gate_up_w[:, hidden_part:]),
        grad_down,
    )


def solution(mesh):
    axes = Axes(mesh)
    rows = axes.rows
    features = P("col", ("dp",) + rows)
    weight = P("col", rows)
    gain = P("col")
    in_specs = (features, gain) + (weight,) * 4 + (gain,) + (weight,) * 3 + (features,)
    out_specs = (features, features, gain) + (weight,) * 4 + (gain,) + (weight,) * 3
    return jax.shard_map(
        functools.partial(per_device, axes),
        mesh=axes.mesh,
        in_specs=in_specs,
        out_specs=out_specs,
        check_vma=False,
    )
```

```python
import functools
import math

import jax
import jax.numpy as jnp
import numpy as np
from jax import lax
from jax.experimental import pallas as pl
from jax.experimental.pallas import tpu as pltpu
from jax.sharding import PartitionSpec as P

MODEL_WIDTH = 960
QUERY_HEADS = 15
KEY_VALUE_HEADS = 5
HEAD_SIZE = 64

GROUP = QUERY_HEADS // KEY_VALUE_HEADS
KEY_VALUE_WIDTH = KEY_VALUE_HEADS * HEAD_SIZE

norm_epsilon = 1e-05
rotary_base = 100000.0
masked_value = -1e30
bf16 = jnp.bfloat16
f32 = jnp.float32


class Axes:
    def __init__(self, mesh):
        shape = dict(mesh.shape)
        inner = shape["row"] // 4
        if inner == 1:
            names, sizes = ("dp", "hi", "core", "col"), (shape["dp"], 2, 2, shape["col"])
            self.pair, self.inner = "core", ()
        else:
            names = ("dp", "hi", "pair", "inner", "core", "col")
            sizes = (shape["dp"], 2, 2, inner // 2, 2, shape["col"])
            self.pair, self.inner = "pair", ("inner", "core")
        self.mesh = jax.sharding.Mesh(mesh.devices.reshape(sizes), names)
        self.names, self.sizes, self.inner_count = names, sizes, inner
        self.rows = names[1:-1]
        self.quarter = ("hi", self.pair)

    def flip(self, value, *flipped):
        grid = np.arange(math.prod(self.sizes)).reshape(self.sizes)
        for name in flipped:
            grid = np.flip(grid, self.names.index(name))
        return lax.ppermute(value, self.names, list(enumerate(grid.ravel().tolist())))

    def swap(self, value):
        grid = np.arange(math.prod(self.sizes)).reshape(self.sizes[0], 4, -1, 4)
        return lax.ppermute(
            value, self.names, list(enumerate(grid.transpose(0, 3, 2, 1).ravel().tolist()))
        )

    def gather_inner(self, value):
        return lax.all_gather(value, self.inner, axis=1, tiled=True) if self.inner else value

    def scatter_inner(self, value):
        if not self.inner:
            return value
        return lax.psum_scatter(value, self.inner, scatter_dimension=1, tiled=True)

    def gather_quarter(self, value):
        far = self.flip(value, "hi")
        near = self.flip(jnp.stack([value, far]), self.pair)
        return [value, near[0], far, near[1]]

    def scatter_quarter(self, blocks):
        near = self.flip(jnp.stack([blocks[1], blocks[3]]).astype(bf16), self.pair)
        far = self.flip((blocks[2] + near[1]).astype(bf16), "hi")
        return blocks[0] + near[0] + far

    def col_xor(self, value, step):
        grid = np.arange(math.prod(self.sizes)).reshape(-1, self.sizes[-1])
        other = grid[:, np.arange(self.sizes[-1]) ^ step]
        return lax.ppermute(value, self.names, list(zip(grid.ravel().tolist(), other.ravel().tolist())))

    def gather_col_steps(self, value):
        far = self.col_xor(value, 2)
        near = self.col_xor(jnp.stack([value, far]), 1)
        return [value, near[0], far, near[1]]

    def scatter_col_steps(self, part):
        blocks = part.reshape(self.sizes[-1], -1, part.shape[1])
        near = self.col_xor(jnp.stack([blocks[1], blocks[3]]).astype(bf16), 1)
        far = self.col_xor((blocks[2] + near[1]).astype(bf16), 2)
        return blocks[0] + near[0] + far

    def dp_sum(self, value):
        return value + self.flip(value.astype(bf16), "dp")

    def exchange_quarter(self, blocks):
        return [
            blocks[0],
            self.flip(blocks[1], self.pair),
            self.flip(blocks[2], "hi"),
            self.flip(blocks[3], "hi", self.pair),
        ]

    def gather_col(self, value):
        count = self.sizes[-1]
        return lax.all_to_all(jnp.broadcast_to(value[None], (count,) + value.shape), "col", 0, 0)

    def by_dp(self, first, second):
        return jnp.where(lax.axis_index("dp") == 0, first, second)

    def gather_half(self, value):
        parts = value.reshape(2, -1, value.shape[1])
        return lax.all_gather(self.by_dp(parts[0], parts[1]), "col", axis=0)

    def whole_rows(self, mine, other):
        return self.by_dp(jnp.concatenate([mine, other]), jnp.concatenate([other, mine]))

    def both_halves(self, mine, other):
        both = self.by_dp(jnp.stack([mine, other], axis=1), jnp.stack([other, mine], axis=1))
        return both.reshape(-1, mine.shape[-1])

    def spread(self, *values):
        count = self.sizes[-1]
        width, tokens = values[0].shape
        parts = jnp.stack(values).reshape(len(values), width, 2 * count, -1)
        parts = jnp.where(lax.axis_index("core") == 1, parts[:, :, ::-1], parts)
        parts = parts.reshape(len(values), width, count, 2, -1).transpose(3, 2, 0, 1, 4)
        parts = parts.reshape((2 * count,) + parts.shape[2:])
        got = lax.all_to_all(parts, ("core", "col"), 0, 0)
        got = got.reshape((2, count) + got.shape[1:])
        return [
            jnp.concatenate([got[part, :, i].reshape(count * width, -1) for part in range(2)], axis=1)
            for i in range(len(values))
        ]

    def pack(self, gains, *values):
        count, rows = self.sizes[-1], gains.shape[0]
        width, size = values[0].shape[0] // count, values[0].shape[1] // 2
        extra_rows = -(-rows * width // (16 * size)) * 16
        extra = gains.astype(bf16).reshape(rows, count, width).transpose(1, 0, 2)
        extra = jnp.pad(
            extra.reshape(count, -1), ((0, 0), (0, extra_rows * size - rows * width))
        ).reshape(count, extra_rows, size)
        parts = jnp.stack(
            [
                jnp.concatenate(
                    [
                        value[j * width : (j + 1) * width, part * size : (part + 1) * size]
                        for value in values
                    ]
                    + [extra[j]]
                )
                for part in range(2)
                for j in range(count)
            ]
        )
        return parts

    def unspread(self, parts, many, rows):
        count = self.sizes[-1]
        size = parts.shape[2]
        width = MODEL_WIDTH // count
        got = lax.all_to_all(parts, ("core", "col"), 0, 0)
        turn = lax.axis_index("core") == 1
        outs = []
        for i in range(many):
            pieces = [got[k * count + j, i * width : (i + 1) * width] for j in range(count) for k in range(2)]
            pieces = [jnp.where(turn, pieces[-1 - j], pieces[j]) for j in range(2 * count)]
            outs.append(jnp.concatenate(pieces, axis=1))
        extra = jnp.sum(got[:, many * width :].astype(f32), axis=0)
        return outs + [extra.reshape(-1)[: rows * width].reshape(rows, width)]


def after(value, *others):
    return lax.optimization_barrier((value,) + others)[0]


together = lax.optimization_barrier


def xor_blocks(blocks, shift):
    step = 1
    while step < len(blocks):
        turn = (shift & step) != 0
        blocks = [jnp.where(turn, blocks[i ^ step], blocks[i]) for i in range(len(blocks))]
        step *= 2
    return blocks


def xor_order(value, shift):
    return jnp.stack(xor_blocks(list(value), shift))


def xor_rows(value, shift):
    return jnp.concatenate(xor_blocks(jnp.split(value, 4), shift))


def rotary_tables(positions):
    half = HEAD_SIZE // 2
    inverse = rotary_base ** (-jnp.arange(half, dtype=f32) * (2.0 / HEAD_SIZE))
    angles = inverse[:, None] * positions.astype(f32)[None, :]
    return (jnp.cos(angles)[None], jnp.sin(angles)[None])


def rotate(value, cosine, sine):
    shaped = value.reshape(-1, 2, HEAD_SIZE // 2, value.shape[1])
    first, second = shaped[:, 0], shaped[:, 1]
    turned = jnp.stack([first * cosine - second * sine, second * cosine + first * sine], axis=1)
    return turned.reshape(value.shape)


def norm_forward(value, gain):
    scale = lax.rsqrt(jnp.sum(value * value, axis=0) / MODEL_WIDTH + norm_epsilon)
    return ((value * scale[None, :] * gain[:, None]).astype(bf16), scale)


def norm_backward(grad_normed, value, scale, gain):
    weighted = grad_normed * gain[:, None]
    inner = jnp.sum(value * weighted, axis=0)
    grad_value = (
        weighted * scale[None, :]
        - value * (scale * scale * scale * inner / MODEL_WIDTH)[None, :]
    )
    return (grad_value, jnp.sum(grad_normed * value * scale[None, :], axis=1))


def dot(left, right, left_axis, right_axis):
    return lax.dot_general(
        left, right, (((left_axis,), (right_axis,)), ((), ())), preferred_element_type=f32
    )


def chunk_blocks(core, col, col_count):
    return ((col, core), (2 * col_count - 1 - col, 1 - core))


def fill_keys(core, col, col_count, own, other, key_s, value_s):
    size = own.shape[3] // 2
    for j in range(col_count):
        for ref, source in ((own, core), (other, 1 - core)):
            for part, (block, side) in enumerate(chunk_blocks(source, col ^ j, col_count)):
                key_s[block, side] = ref[j, 0, :, part * size : (part + 1) * size]
                value_s[block, side] = ref[j, 1, :, part * size : (part + 1) * size]


def both_sides(scratch, block):
    return jnp.concatenate([scratch[block, 0], scratch[block, 1]], axis=1)


def side_by_side(ref, part, size):
    return jnp.concatenate(
        [
            ref[g * HEAD_SIZE : (g + 1) * HEAD_SIZE, part * size : (part + 1) * size]
            for g in range(GROUP)
        ],
        axis=1,
    )


def tile_allowed(shape, size, part, block, early, late):
    start = jnp.where(part == 0, 2 * early[0] + early[1], 2 * late[0] + late[1]) * size
    lane = lax.rem(lax.broadcasted_iota(jnp.int32, shape, 1), size)
    return lax.broadcasted_iota(jnp.int32, shape, 0) - lane <= start - block * 2 * size


def attend_kernel(col_count, place, query, own, other, output, logsum, *scratch):
    key_s, value_s, query_s, score_s, sum_s, total_s = scratch
    core, col = place[0], place[1]
    size = query.shape[1] // 2
    fill_keys(core, col, col_count, own, other, key_s, value_s)
    early, late = chunk_blocks(core, col, col_count)
    for part in range(2):
        query_s[part] = side_by_side(query, part, size)
    sum_s[...] = jnp.zeros_like(sum_s)
    total_s[...] = jnp.zeros_like(total_s)
    shape = score_s.shape[1:]
    top = [jnp.full((1, shape[1]), masked_value, f32) for _ in range(2)]
    tiles = []
    for tile in range(2 * col_count + 1):
        part = (tile > early[0]).astype(jnp.int32)
        block = tile - part * (early[0] + 1)
        tiles.append((part, block))
        scores = dot(both_sides(key_s, block), query_s[part], 0, 0)
        scores = jnp.where(
            tile_allowed(shape, size, part, block, early, late), scores, masked_value
        )
        score_s[tile] = scores
        high = jnp.max(scores, axis=0, keepdims=True)
        for side in range(2):
            top[side] = jnp.where(part == side, jnp.maximum(top[side], high), top[side])
    for tile, (part, block) in enumerate(tiles):
        weights = jnp.exp(score_s[tile] - jnp.where(part == 0, top[0], top[1]))
        total_s[part] += jnp.broadcast_to(
            jnp.sum(weights, axis=0, keepdims=True), total_s.shape[1:]
        )
        sum_s[part] += dot(both_sides(value_s, block), weights.astype(bf16), 1, 0)
    for part in range(2):
        total = total_s[part][:1]
        out = (sum_s[part] * (1.0 / total)).astype(bf16)
        for g in range(GROUP):
            output[g * HEAD_SIZE : (g + 1) * HEAD_SIZE, part * size : (part + 1) * size] = out[
                :, g * size : (g + 1) * size
            ]
        logsum[0, part : part + 1, :] = top[part] + jnp.log(total)


def attend_back_kernel(col_count, place, query, grad, output, logsum, own, other, *refs):
    grad_query, grad_own, grad_other = refs[:3]
    key_s, value_s, query_s, grad_s, inner_s, sum_query, sum_key, sum_value = refs[3:]
    core, col = place[0], place[1]
    size = query.shape[1] // 2
    fill_keys(core, col, col_count, own, other, key_s, value_s)
    early, late = chunk_blocks(core, col, col_count)
    for part in range(2):
        query_s[part] = side_by_side(query, part, size)
        grad_part = side_by_side(grad, part, size)
        grad_s[part] = grad_part
        inner = jnp.sum(
            grad_part.astype(f32) * side_by_side(output, part, size).astype(f32),
            axis=0,
            keepdims=True,
        )
        wide = (8, inner.shape[1])
        inner_s[part] = jnp.concatenate(
            [
                jnp.broadcast_to(inner, wide),
                jnp.broadcast_to(logsum[0, part : part + 1, :], wide),
            ],
            axis=0,
        )
    sum_query[...] = jnp.zeros_like(sum_query)
    sum_key[...] = jnp.zeros_like(sum_key)
    sum_value[...] = jnp.zeros_like(sum_value)
    shape = (2 * size, GROUP * size)
    for tile in range(2 * col_count + 1):
        part = (tile > early[0]).astype(jnp.int32)
        block = tile - part * (early[0] + 1)
        key, value = both_sides(key_s, block), both_sides(value_s, block)
        query_part, grad_part = query_s[part], grad_s[part]
        inner = inner_s[part]
        scores = jnp.where(
            tile_allowed(shape, size, part, block, early, late),
            dot(key, query_part, 0, 0),
            masked_value,
        )
        probs = jnp.exp(scores - inner[8:9])
        grad_probs = dot(value, grad_part, 0, 0)
        grad_scores = (probs * (grad_probs - inner[:1])).astype(bf16)
        sum_value[block] += dot(grad_part, probs.astype(bf16), 1, 1)
        sum_key[block] += dot(query_part, grad_scores, 1, 1)
        sum_query[part] += dot(key, grad_scores, 1, 0)
    for part in range(2):
        out = sum_query[part] * (1.0 / math.sqrt(HEAD_SIZE))
        for g in range(GROUP):
            grad_query[g * HEAD_SIZE : (g + 1) * HEAD_SIZE, part * size : (part + 1) * size] = out[
                :, g * size : (g + 1) * size
            ]
    for j in range(col_count):
        for ref, source in ((grad_own, core), (grad_other, 1 - core)):
            for part, (block, side) in enumerate(chunk_blocks(source, col ^ j, col_count)):
                for index, total in enumerate((sum_key, sum_value)):
                    whole = total[block]
                    ref[j, index, :, part * size : (part + 1) * size] = jnp.where(
                        side == 0, whole[:, :size], whole[:, size:]
                    ).astype(ref.dtype)


def attention_specs(tokens, col_count):
    heads = pl.BlockSpec((GROUP * HEAD_SIZE, tokens), lambda h: (h, 0))
    pair = pl.BlockSpec((col_count, 2, HEAD_SIZE, tokens), lambda h: (0, 0, h, 0))
    lanes = GROUP * tokens // 2
    logsum = pl.BlockSpec((1, 2, lanes), lambda h: (h, 0, 0))
    place = pl.BlockSpec(memory_space=pltpu.SMEM)
    keys = [pltpu.VMEM((2 * col_count, 2, HEAD_SIZE, tokens // 2), bf16)] * 2
    return heads, pair, logsum, place, lanes, keys


def attend(place, query, own, other, col_count):
    tokens = query.shape[1]
    count = 2 * col_count
    heads, pair, logsum, place_spec, lanes, keys = attention_specs(tokens, col_count)
    return pl.pallas_call(
        functools.partial(attend_kernel, col_count),
        grid=(KEY_VALUE_HEADS,),
        in_specs=[place_spec, heads, pair, pair],
        out_specs=[heads, logsum],
        out_shape=[
            jax.ShapeDtypeStruct(query.shape, bf16),
            jax.ShapeDtypeStruct((KEY_VALUE_HEADS, 2, lanes), f32),
        ],
        scratch_shapes=keys
        + [
            pltpu.VMEM((2, HEAD_SIZE, lanes), bf16),
            pltpu.VMEM((count + 1, tokens, lanes), f32),
            pltpu.VMEM((2, HEAD_SIZE, lanes), f32),
            pltpu.VMEM((2, 8, lanes), f32),
        ],
        compiler_params=pltpu.CompilerParams(vmem_limit_bytes=32 * 2**20),
        cost_estimate=pl.CostEstimate(
            flops=KEY_VALUE_HEADS * (count + 1) * tokens * lanes * HEAD_SIZE * 8,
            bytes_accessed=4 * 2**20,
            transcendentals=KEY_VALUE_HEADS * (count + 1) * tokens * lanes,
        ),
        name="attend",
    )(place, query, own, other)


def attend_back(place, query, grad, output, logsum, own, other, col_count):
    tokens = query.shape[1]
    count = 2 * col_count
    heads, pair, logsum_spec, place_spec, lanes, keys = attention_specs(tokens, col_count)
    return pl.pallas_call(
        functools.partial(attend_back_kernel, col_count),
        grid=(KEY_VALUE_HEADS,),
        in_specs=[place_spec, heads, heads, heads, logsum_spec, pair, pair],
        out_specs=[heads, pair, pair],
        out_shape=[
            jax.ShapeDtypeStruct(query.shape, f32),
            jax.ShapeDtypeStruct(own.shape, f32),
            jax.ShapeDtypeStruct(own.shape, bf16),
        ],
        scratch_shapes=keys
        + [
            pltpu.VMEM((2, HEAD_SIZE, lanes), bf16),
            pltpu.VMEM((2, HEAD_SIZE, lanes), bf16),
            pltpu.VMEM((2, 16, lanes), f32),
            pltpu.VMEM((2, HEAD_SIZE, lanes), f32),
            pltpu.VMEM((count, HEAD_SIZE, tokens), f32),
            pltpu.VMEM((count, HEAD_SIZE, tokens), f32),
        ],
        compiler_params=pltpu.CompilerParams(vmem_limit_bytes=32 * 2**20),
        cost_estimate=pl.CostEstimate(
            flops=KEY_VALUE_HEADS * (count + 1) * tokens * lanes * HEAD_SIZE * 20,
            bytes_accessed=8 * 2**20,
            transcendentals=KEY_VALUE_HEADS * (count + 1) * tokens * lanes,
        ),
        name="attend_back",
    )(place, query, grad, output, logsum, own, other)


def per_device(
    axes,
    tokens,
    attn_gain,
    w_query,
    key_weight,
    value_weight,
    w_output,
    mlp_gain,
    w_gate,
    w_up,
    w_down,
    cotangent,
):
    col_count = axes.sizes[-1]
    core, col = lax.axis_index("core"), lax.axis_index("col")
    quarter = lax.axis_index("hi") * 2 + lax.axis_index(axes.pair)
    w_query, key_weight, value_weight, w_output, w_gate, w_up, w_down = (
        axes.gather_inner(item)
        for item in (w_query, key_weight, value_weight, w_output, w_gate, w_up, w_down)
    )
    local_dim = tokens.shape[0]
    query_part, pair_part = w_query.shape[1], key_weight.shape[1]
    hidden_part = w_gate.shape[1]

    (inputs,) = axes.spread(tokens)
    inputs = inputs.astype(f32)
    down_block = axes.swap(w_down.T)
    pair_block = jnp.concatenate(
        [key_weight, value_weight, attn_gain[:, None], mlp_gain[:, None]], axis=1
    )
    pair_col = jnp.concatenate(xor_blocks(axes.gather_col_steps(pair_block), col))
    wide_block = jnp.concatenate([w_query, w_output], axis=1)
    inputs, pair_col, down_block, wide_far = together(
        (inputs, pair_col, down_block, axes.col_xor(wide_block, 2))
    )
    gains = pair_col[:, 2 * pair_part :].astype(f32)
    gain_one, gain_two = gains[:, 0], gains[:, 1]

    tokens_here = inputs.shape[1]
    (grad_top,) = axes.spread(after(cotangent, inputs))
    act_one, scale_one = norm_forward(inputs, gain_one)
    pair_far, pair_close, wide_near, act_one = together(
        (
            axes.flip(pair_col, "hi"),
            axes.flip(pair_col, axes.pair),
            axes.col_xor(jnp.stack([wide_block, wide_far]), 1),
            act_one,
        )
    )

    size = tokens_here // 2
    steps = jnp.arange(size)
    early, late = chunk_blocks(core, col, col_count)
    positions = jnp.concatenate(
        [(2 * early[0] + early[1]) * size + steps, (2 * late[0] + late[1]) * size + steps]
    )
    cosine, sine = rotary_tables(positions)
    pair_last = axes.flip(pair_far, axes.pair)
    pair_weight = jnp.stack([pair_col, pair_close, pair_far, pair_last])
    pair_weight = pair_weight[:, :, : 2 * pair_part]
    pair = xor_order(
        jnp.einsum("jdf,dt->jft", pair_weight, act_one, preferred_element_type=f32).astype(bf16),
        quarter,
    )
    key = pair[:, :pair_part].reshape(KEY_VALUE_WIDTH, -1)
    value = pair[:, pair_part:].reshape(KEY_VALUE_WIDTH, -1)
    key = rotate(key.astype(f32), cosine, sine).astype(bf16)
    pair, grad_top = together((jnp.stack([key, value]), grad_top))
    wide_col = xor_blocks([wide_block, wide_near[0], wide_far, wide_near[1]], col)
    query_col = jnp.concatenate([block[:, :query_part] for block in wide_col])
    output_col = jnp.concatenate([block[:, query_part:] for block in wide_col])
    query_col, output_col = together((query_col, output_col))

    pair_z_far, query_far = together((axes.col_xor(pair, 2), axes.flip(query_col, "hi")))
    gate_up_mine = axes.gather_half(after(jnp.concatenate([w_gate, w_up], axis=1), pair_z_far))

    query_near = axes.flip(jnp.stack([query_col, query_far]), axes.pair)
    query_weight = jnp.stack([query_col, query_near[0], query_far, query_near[1]])
    query = xor_order(
        jnp.einsum("jdf,dt->jft", query_weight, act_one, preferred_element_type=f32).astype(bf16),
        quarter,
    ).reshape(MODEL_WIDTH, -1)
    query = (
        rotate(query.astype(f32), cosine, sine).astype(bf16) * (1.0 / math.sqrt(HEAD_SIZE))
    ).astype(bf16)
    pair_z_near, output_far, query = together(
        (
            axes.col_xor(jnp.stack([pair, pair_z_far]), 1),
            axes.flip(after(output_col, query_far), "hi"),
            query,
        )
    )

    down_weight = lax.all_gather(after(down_block, query), "col", axis=0, tiled=True)
    own = jnp.stack([pair, pair_z_near[0], pair_z_far, pair_z_near[1]])
    other, output_near = together(
        (
            axes.flip(own, "core"),
            axes.flip(jnp.stack([output_col, output_far]), axes.pair),
        )
    )
    output_weight = jnp.stack(
        xor_blocks([output_col, output_near[0], output_far, output_near[1]], quarter)
    )

    place = jnp.stack([core, col]).astype(jnp.int32)
    attended, logsum = attend(place, query, own, other, col_count)
    gate_up_other = axes.flip(after(gate_up_mine, query), "dp")
    attended, grad_far = together((attended, axes.flip(after(grad_top, other), "hi")))

    resid = inputs + jnp.einsum(
        "rfd,ft->rdt", output_weight, attended, preferred_element_type=f32
    ).reshape(inputs.shape)
    act_two, scale_two = norm_forward(resid, gain_two)
    grad_near = axes.flip(jnp.stack([grad_top, grad_far]), axes.pair)
    grad_branch = jnp.concatenate([grad_top, grad_near[0], grad_far, grad_near[1]], axis=1)
    gate_up_weight = axes.both_halves(gate_up_mine, gate_up_other)
    act_two, act_two_far, act_two_near, grad_branch, gate_up_weight = together(
        (
            act_two,
            axes.flip(act_two, "hi"),
            axes.flip(act_two, axes.pair),
            grad_branch,
            gate_up_weight,
        )
    )
    act_two_last, down_weight = together((axes.flip(act_two_far, axes.pair), down_weight))

    act_two_all = jnp.concatenate(
        [act_two, act_two_near, act_two_far, act_two_last], axis=1
    )
    act_two_all = lax.optimization_barrier(act_two_all)
    grad_hidden = dot(down_weight, grad_branch, 0, 0)
    gate_up_vals = dot(gate_up_weight, act_two_all, 0, 0)
    gate_vals, up_vals = gate_up_vals[:hidden_part], gate_up_vals[hidden_part:]
    sigmoid = jax.nn.sigmoid(gate_vals)
    silu_vals = gate_vals * sigmoid
    hidden = (silu_vals * up_vals).astype(bf16)
    grad_gate_up = jnp.concatenate(
        [
            grad_hidden * up_vals * (sigmoid * (1.0 + gate_vals * (1.0 - sigmoid))),
            grad_hidden * silu_vals,
        ],
        axis=0,
    ).astype(bf16)
    hidden, grad_gate_up = together((hidden, grad_gate_up))

    def token_blocks(value):
        return [value[:, i * tokens_here : (i + 1) * tokens_here] for i in range(4)]

    parts = token_blocks(dot(gate_up_weight, grad_gate_up, 1, 0))
    near = axes.flip(jnp.stack([parts[1], parts[3]]).astype(bf16), axes.pair)
    act_two_rel = lax.optimization_barrier(xor_rows(act_two_all, col))
    gate_up_part = dot(act_two_rel, grad_gate_up, 1, 1)
    gate_up_part = gate_up_part.reshape(col_count, local_dim, -1)
    gate_up_low = jnp.stack([gate_up_part[1], gate_up_part[3]]).astype(bf16)
    near, gate_up_low, act_one_far = together(
        (near, gate_up_low, axes.flip(after(act_one, act_two_last), "hi"))
    )
    gate_up_near = axes.col_xor(gate_up_low, 1)
    down_w_part = dot(grad_branch, hidden, 1, 1).astype(bf16)
    far, down_w_part = together(
        (axes.flip((parts[2] + near[1]).astype(bf16), "hi"), down_w_part)
    )
    down_sum = lax.psum_scatter(down_w_part, "col", scatter_dimension=0, tiled=True)
    grad_act_two = parts[0] + near[0] + far
    grad_resid_norm, gain_two_part = norm_backward(grad_act_two, resid, scale_two, gain_two)
    grad_resid = grad_top.astype(f32) + grad_resid_norm
    grad_attn = grad_resid.astype(bf16)
    grad_attended = jnp.einsum(
        "rfd,rdt->ft",
        output_weight,
        grad_attn.reshape(4, -1, tokens_here),
        preferred_element_type=f32,
    ).astype(bf16)

    grad_attn_far = axes.flip(grad_attn, "hi")
    grad_query, grad_own, grad_other = attend_back(
        place, query, grad_attended, attended, logsum, own, other, col_count
    )
    grad_other, gate_up_near = together((grad_other, gate_up_near))
    gate_up_low = (gate_up_part[2] + gate_up_near[1]).astype(bf16)
    grad_pair = grad_own + axes.flip(grad_other, "core")
    pair_low = jnp.stack([grad_pair[1], grad_pair[3]]).astype(bf16)
    pair_low, gate_up_low = together((pair_low, gate_up_low))

    grad_query = rotate(grad_query, cosine, -sine).astype(bf16)
    query_rel = xor_order(grad_query.reshape(4, -1, tokens_here), quarter)
    parts = token_blocks(dot(down_weight, after(hidden, pair_low), 1, 0))
    near = axes.flip(jnp.stack([parts[1], parts[3]]).astype(bf16), axes.pair)
    attended_rel = xor_order(attended.reshape(4, -1, tokens_here), quarter)
    sent = jnp.concatenate([query_rel, attended_rel], axis=1)
    pair_near, near, head_all, grad_attn_far, gate_up_far = together(
        (
            axes.col_xor(pair_low, 1),
            near,
            axes.exchange_quarter(list(after(sent, pair_low))),
            grad_attn_far,
            axes.col_xor(gate_up_low, 2),
        )
    )
    both_blocks = jnp.stack([act_one, grad_attn, act_one_far, grad_attn_far])
    both_near = axes.flip(both_blocks, axes.pair)
    pair_low = (grad_pair[2] + pair_near[1]).astype(bf16)
    head_all = jnp.concatenate(head_all, axis=1)
    act_one_all, grad_attn_all = (
        jnp.concatenate(
            [both_blocks[i], both_near[i], both_blocks[2 + i], both_near[2 + i]], axis=1
        )
        for i in range(2)
    )
    act_one_rel, grad_attn_rel = together(
        (xor_rows(act_one_all, col), xor_rows(grad_attn_all, col))
    )
    grad_query_w = dot(act_one_rel, head_all[:query_part], 1, 1)
    grad_output_w = dot(grad_attn_rel, head_all[query_part:], 1, 1)
    grad_act_one = jnp.einsum(
        "jdf,jft->dt", query_weight, after(query_rel, pair_low), preferred_element_type=f32
    )
    early_part = [
        item.reshape(col_count, 2, local_dim // 2, -1) for item in (grad_query_w, grad_output_w)
    ]
    early_sent = jnp.stack([axes.by_dp(item[:, 1], item[:, 0]).astype(bf16) for item in early_part])
    early_kept = jnp.stack([axes.by_dp(item[:, 0], item[:, 1]) for item in early_part])
    pair_far, far, early_got, early_kept, grad_act_one, act_one_rel = together(
        (
            axes.col_xor(pair_low, 2),
            axes.flip((parts[2] + near[1]).astype(bf16), "hi"),
            axes.flip(early_sent, "dp"),
            early_kept,
            grad_act_one,
            act_one_rel,
        )
    )
    early_part = early_kept + early_got
    output = (resid + (parts[0] + near[0] + far)).astype(bf16)
    grad_pair = grad_pair[0] + pair_near[0] + pair_far

    grad_key = rotate(grad_pair[0], cosine, -sine).astype(bf16)
    grad_value = grad_pair[1].astype(bf16)
    pair_rel = xor_order(
        jnp.concatenate(
            [grad_key.reshape(4, -1, tokens_here), grad_value.reshape(4, -1, tokens_here)], axis=1
        ),
        quarter,
    )
    grad_act_one = grad_act_one + jnp.einsum(
        "jdf,jft->dt", pair_weight, pair_rel, preferred_element_type=f32
    )
    grad_inputs_norm, gain_one_part = norm_backward(grad_act_one, inputs, scale_one, gain_one)
    grad_inputs = (grad_resid + grad_inputs_norm).astype(bf16)
    parts = axes.pack(jnp.stack([gain_one_part, gain_two_part]), output, grad_inputs)
    pair_all, parts, down_sum, early_near = together(
        (
            axes.exchange_quarter(list(pair_rel)),
            parts,
            axes.swap(after(down_sum, grad_pair)),
            axes.col_xor(jnp.stack([early_part[:, 1], early_part[:, 3]]).astype(bf16), 1),
        )
    )
    output, input_grad, gain_sum = axes.unspread(parts, 2, 2)
    grad_pair_w = dot(act_one_rel, jnp.concatenate(pair_all, axis=1), 1, 1)
    late_part = grad_pair_w.reshape(col_count, local_dim, -1)
    gate_up_total = gate_up_part[0] + gate_up_near[0] + gate_up_far
    late_near, down_dp, early_far, gate_up_dp = together(
        (
            axes.col_xor(jnp.stack([late_part[1], late_part[3]]).astype(bf16), 1),
            axes.flip(after(down_sum, grad_pair_w), "dp"),
            axes.col_xor(after((early_part[:, 2] + early_near[1]).astype(bf16), grad_pair_w), 2),
            axes.flip(after(gate_up_total.astype(bf16), grad_pair_w), "dp"),
        )
    )
    early_sum = (early_part[:, 0] + early_near[0] + early_far).astype(bf16)
    query_half, output_half = early_sum[0], early_sum[1]
    late_far, query_dp, output_half = together(
        (
            axes.col_xor((late_part[2] + late_near[1]).astype(bf16), 2),
            axes.flip(query_half, "dp"),
            axes.swap(output_half),
        )
    )
    late_sum = late_part[0] + late_near[0] + late_far
    late_dp, output_dp, gain_sum = together(
        (
            axes.flip(late_sum.astype(bf16), "dp"),
            axes.flip(output_half, "dp"),
            gain_sum,
        )
    )
    gain_sum = gain_sum + axes.flip(gain_sum, "hi")
    gain_sum = gain_sum + axes.flip(gain_sum, "dp")
    for name in axes.rows[1:-1]:
        gain_sum = lax.psum(gain_sum, name)
    grad_gate_up_w = gate_up_total + gate_up_dp
    grad_pair_w = late_sum + late_dp
    grad_query_w = axes.whole_rows(query_half, query_dp).astype(f32)
    grad_output = axes.whole_rows(output_half, output_dp).T.astype(f32)
    grad_output = axes.scatter_inner(grad_output)
    grad_down = axes.scatter_inner((down_sum.astype(f32) + down_dp).T)

    return (
        output,
        input_grad.astype(f32),
        gain_sum[0],
        axes.scatter_inner(grad_query_w),
        axes.scatter_inner(grad_pair_w[:, :pair_part]),
        axes.scatter_inner(grad_pair_w[:, pair_part:]),
        grad_output,
        gain_sum[1],
        axes.scatter_inner(grad_gate_up_w[:, :hidden_part]),
        axes.scatter_inner(grad_gate_up_w[:, hidden_part:]),
        grad_down,
    )


def solution(mesh):
    axes = Axes(mesh)
    rows = axes.rows
    features = P("col", ("dp",) + rows)
    weight = P("col", rows)
    gain = P("col")
    in_specs = (features, gain) + (weight,) * 4 + (gain,) + (weight,) * 3 + (features,)
    out_specs = (features, features, gain) + (weight,) * 4 + (gain,) + (weight,) * 3
    return jax.shard_map(
        functools.partial(per_device, axes),
        mesh=axes.mesh,
        in_specs=in_specs,
        out_specs=out_specs,
        check_vma=False,
    )
```
